512 devices in a mesh: lon: 32 (over x, y), lat: 16 (over z, core).
Axes of the slice: x: 4, y: 8, z: 8, core: 2. Of those that a mesh axis runs over, the one named last changes fastest.
Arguments:
- tracer: float32 [2, 25, 128, 4096], P(None, None, 'lat', 'lon'), may hold values from -6 to 6
- ocean_mask: int32 [25, 128, 4096], P(None, 'lat', 'lon'), may hold values from 0 to 1, as said below
- kappa_lon: bfloat16 [25, 128, 4096], P(None, 'lat', 'lon'), may hold values from 0.049804688 to 0.23925781
- kappa_lat: bfloat16 [25, 128, 4096], P(None, 'lat', 'lon'), may hold values from 4 to 256
- vertical_root: float32 [2, 25, 25], replicated, may hold values from -1.25 to 1.25
Outputs:
- correlated: float32 [2, 25, 128, 4096], P(None, None, 'lat', 'lon')
The draws below stay inside these ranges and needn't reach their ends.
Inputs may be any that keep to these rules, and one draw needn't show every extreme that they name: `ocean_mask`: 0 or 1; a cell that is land at one level is land at every deeper level.
All inputs are finite; a program needn't handle non-finite values.
Results may differ from the reference program's by a relative error of at most 0.0003.
Values sent between devices are 32-bit elements; how exact they have to be, the bound alone decides.
A program may use at most 64 MiB of HBM per device.

```python
import math
import jax
import jax.numpy as jnp
from jax import lax

LEV = 25
FIELDS = 2
STEPS = 4
NX = 4096
NY = 128


def draw_ocean_mask(key, part):
    subkeys = jax.random.split(key, 5)
    row_start = jax.random.randint(subkeys[0], (8,), 0, NY)
    row_extent = jax.random.randint(subkeys[1], (8,), max(NY // 16, 1), max(NY // 4, 2))
    col_start = jax.random.randint(subkeys[2], (8,), 0, NX)
    col_extent = jax.random.randint(subkeys[3], (8,), max(NX // 16, 1), max(NX // 4, 2))
    rows_all = jnp.arange(NY, dtype=jnp.int32)
    cols_all = jnp.arange(NX, dtype=jnp.int32)
    in_rows = (rows_all[None, :] - row_start[:, None]) % NY < row_extent[:, None]
    in_cols = (cols_all[None, :] - col_start[:, None]) % NX < col_extent[:, None]
    land = jnp.any(in_rows[:, :, None] & in_cols[:, None, :], axis=0)
    depth = jax.random.randint(subkeys[4], (NY, NX), LEV // 2, LEV + 1)
    levels = jnp.arange(LEV, dtype=jnp.int32)[:, None, None]
    sea = (levels < depth[None]) & jnp.logical_not(land)[None]
    return sea.astype(jnp.int32)


def level_of(stream_key, shape, cuts, least, largest):
    def one(position, blocks):
        heights = jax.random.uniform(jax.random.fold_in(jax.random.fold_in(stream_key, 6), position), (blocks,), jnp.float32, least / len(cuts), largest / len(cuts))
        return jnp.repeat(jnp.exp(heights), shape[position] // blocks).reshape((-1,) + (1,) * (len(shape) - position - 1))

    level = one(*cuts[0])
    for cut in cuts[1:]:
        level = level * one(*cut)
    return level


def normal_values(rng, shape, width, reach, shards=(), held_as=jnp.bfloat16):
    factor_of = level_of(rng, shape, shards, -0.22, 0.18) if shards else 1.0
    result = jax.random.normal(rng, shape, jnp.float32) * width * factor_of
    return jnp.minimum(jnp.maximum(result, -reach), reach).astype(held_as)


def setup_inputs(seed: int = 0) -> dict:
    key_of = jax.random.split(jax.random.key(seed), 6)
    return {
        "tracer": normal_values(key_of[0], (FIELDS, LEV, NY, NX), 1.0, 6.0, ((2, 16), (3, 32)), jnp.float32),
        "ocean_mask": draw_ocean_mask(jax.random.fold_in(key_of[5], 71), 0),
        "kappa_lon": jnp.clip(0.049804688 + 0.18945312 * jax.random.uniform(key_of[2], (LEV, NY, NX), jnp.float32) ** level_of(key_of[2], (LEV, NY, NX), ((1, 16), (2, 32)), -0.2, 0.2), 0.049804688, 0.23925781).astype(jnp.bfloat16),
        "kappa_lat": jnp.clip(jnp.exp(math.log(256.0) - 4.158883 * jax.random.uniform(key_of[3], (LEV, NY, NX), jnp.float32) ** level_of(key_of[3], (LEV, NY, NX), ((1, 16), (2, 32)), -0.2, 0.2)), 4.0, 256.0).astype(jnp.bfloat16),
        "vertical_root": normal_values(key_of[4], (FIELDS, LEV, LEV), LEV ** -0.5, 1.25, (), jnp.float32),
    }


def lon_diffuse(state, coefficient):
    for sweep in range(STEPS):
        face_east = jnp.minimum(coefficient, jnp.roll(coefficient, -1, axis=3))
        east_flux = face_east * (jnp.roll(state, -1, axis=3) - state)
        state = state + east_flux - jnp.roll(east_flux, 1, axis=3)
    return state


def thomas_solve(values, coefficient):
    padded = jnp.pad(coefficient, ((0, 0), (0, 0), (1, 1), (0, 0)))
    upper_face = jnp.minimum(padded[:, :, 1:-1], padded[:, :, 2:])
    lower_face = jnp.minimum(padded[:, :, :-2], padded[:, :, 1:-1])
    diagonal = 1.0 + lower_face + upper_face

    def forward(carried, inputs):
        ratio_prev, reduced_prev = carried
        lower_row, upper_row, diag_row, value_row = inputs
        denominator = diag_row - lower_row * ratio_prev
        ratio_row = upper_row / denominator
        reduced_row = (value_row + lower_row * reduced_prev) / denominator
        return (ratio_row, reduced_row), (ratio_row, reduced_row)

    start_state = (jnp.zeros((1, values.shape[1], values.shape[3]), jnp.float32),
                   jnp.zeros((values.shape[0], values.shape[1], values.shape[3]), jnp.float32))
    moved = tuple(jnp.moveaxis(item, 2, 0) for item in (lower_face, upper_face, diagonal, values))
    unused, (ratios, reduced) = lax.scan(forward, start_state, moved)

    def backward(next_value, inputs):
        ratio_row, reduced_row = inputs
        current = reduced_row + ratio_row * next_value
        return current, current

    last_value = jnp.zeros((values.shape[0], values.shape[1], values.shape[3]), jnp.float32)
    unused, solved = lax.scan(backward, last_value, (ratios, reduced), reverse=True)
    return jnp.moveaxis(solved, 0, 2)


def reference(tracer, ocean_mask, kappa_lon, kappa_lat, vertical_root):
    ocean = ocean_mask.astype(jnp.float32)[None]
    state = tracer * ocean
    coef_lon = kappa_lon.astype(jnp.float32)[None] * ocean
    coef_lat = kappa_lat.astype(jnp.float32)[None] * ocean
    state = lon_diffuse(state, coef_lon)
    state = thomas_solve(state, coef_lat)
    mixed = jnp.einsum("flk,fkyx->flyx", vertical_root, state, precision=lax.Precision.HIGHEST)
    return mixed * ocean
```

```python
import functools

import jax
import jax.numpy as jnp
from jax import lax
from jax.experimental import pallas as pl
from jax.experimental.pallas import tpu as pltpu
from jax.sharding import PartitionSpec as P

LEV = 25
FIELDS = 2
STEPS = 4
ROWS = 8
LANES = 128
HALF = 13
PAD = HALF + 16
MESH = pl.DeviceIdType.MESH
F32 = jnp.float32
BF16 = jnp.bfloat16


def roll(cells, shift):
    return pltpu.roll(cells, shift % LANES, axis=cells.ndim - 1)


def by_level(ref, half, row):
    return ref[pl.ds(half * HALF * ROWS + row, 16, stride=ROWS), :]


def diffuse(state, face_east, face_west):
    for _ in range(STEPS):
        state = state + (
            face_east * (roll(state, -1) - state) - face_west * (state - roll(state, 1))
        )
    return state


def kernel(
    n_lon, n_lat,
    tr_h, mk_h, kl_h, kt_h, vr_h, out,
    tr, mk, kl, kt, vr,
    lon_s, halo_out, halo_in, inner, lat_s, diff_s, ocean_s,
    ratio_s, ipiv_s, g1_s, g8_s, part_s,
    msg_g, got_g, msg_p, got_p, msg_f, got_f, twice_s, vpad, x_s,
    in_sem, halo_ss, halo_rs, g_ss, g_rs, p_ss, p_rs, f_ss, f_rs,
):
    lon, lat = lax.axis_index("lon"), lax.axis_index("lat")
    east, west = lax.rem(lon + 1, n_lon), lax.rem(lon + n_lon - 1, n_lon)
    solver = lat < HALF

    loads = [
        pltpu.make_async_copy(src, dst, in_sem.at[i])
        for i, (src, dst) in enumerate(
            ((mk_h, mk), (kl_h, kl), (tr_h, tr), (kt_h, kt), (vr_h, vr))
        )
    ]
    for load in loads:
        load.start()

    barrier = pltpu.get_barrier_semaphore()
    for side in (east, west):
        pl.semaphore_signal(barrier, inc=1, device_id={"lon": side}, device_id_type=MESH)

    @pl.loop(1, n_lat)
    def _(d):
        pl.semaphore_signal(
            barrier, inc=1, device_id={"lat": lax.rem(lat + d, n_lat)}, device_id_type=MESH
        )

    lane = lax.broadcasted_iota(jnp.int32, (ROWS, LANES), 1)
    group = lane >> 4
    slot = (lane >> 2) & 3

    def pick(mask, yes, no):
        return jnp.where(jnp.broadcast_to(mask, yes.shape), yes, no)

    got_f[pl.ds(HALF * ROWS, 3 * ROWS), :] = jnp.zeros((3 * ROWS, LANES), F32)
    vpad[...] = jnp.zeros(vpad.shape, F32)
    lat_s[pl.ds(LEV * ROWS, (PAD - LEV) * ROWS), :] = jnp.zeros(((PAD - LEV) * ROWS, LANES), F32)
    for f in range(FIELDS):
        diff_s[f, pl.ds(LEV * ROWS, (PAD - LEV) * ROWS), :] = jnp.zeros(
            ((PAD - LEV) * ROWS, LANES), F32
        )

    loads[0].wait()
    loads[1].wait()
    loads[2].wait()
    for t in range(4):
        n = min(ROWS, LEV - ROWS * t)
        levels = pl.ds(ROWS * t, n)
        ocean = mk[levels].astype(F32)
        ocean_s[pl.ds(ROWS * ROWS * t, n * ROWS), :] = ocean.reshape(n * ROWS, LANES)
        lon_s[0, t, pl.ds(0, n)] = kl[levels].astype(F32) * ocean
        for f in range(FIELDS):
            lon_s[1 + f, t, pl.ds(0, n)] = tr[f, levels] * ocean
    edges = roll(lon_s[:, 0:3, 0], 8)
    for g in range(1, 8):
        edges = pick(group == g, roll(lon_s[:, 0:3, g], 16 * g + 8), edges)
    packed = [edges[:, 0], edges[:, 1], edges[:, 2], roll(lon_s[:, 3, 0], 8)]
    to_east, to_west = roll(packed[0], -4), roll(packed[0], -8)
    for t in range(1, 4):
        to_east = pick(slot == t, roll(packed[t], 4 * t - 4), to_east)
        to_west = pick(slot == t, roll(packed[t], 4 * t - 8), to_west)
    halo_out[0] = to_east
    halo_out[1] = to_west

    pl.semaphore_wait(barrier, n_lat + 1)
    halos = [
        pltpu.make_async_remote_copy(
            src_ref=halo_out.at[i], dst_ref=halo_in.at[i],
            send_sem=halo_ss.at[i], recv_sem=halo_rs.at[i],
            device_id={"lon": side}, device_id_type=MESH,
        )
        for i, side in enumerate((east, west))
    ]
    for halo in halos:
        halo.start()

    loads[3].wait()
    lat_s[pl.ds(0, LEV * ROWS), :] = kt[...].astype(F32).reshape(LEV * ROWS, LANES) * ocean_s[...]
    coef = [jnp.stack([by_level(lat_s, h, y) for h in range(2)]) for y in range(ROWS)]
    ones = jnp.ones_like(coef[0])
    excess = jnp.zeros_like(ones)
    ratio, ipiv, first = [], [], [ones]
    for y in range(ROWS):
        if y < ROWS - 1:
            face = jnp.minimum(coef[y], coef[y + 1])
            inverse = 1.0 / (1.0 + face + excess)
            ratio.append(face * inverse)
            excess = ratio[y] * (1.0 + excess)
            first.append(ratio[y] * first[y])
            ratio_s[y] = ratio[y]
        else:
            inverse = 1.0 / (1.0 + excess)
        ipiv.append(inverse)
        ipiv_s[y] = inverse
    g1, g8 = first[ROWS - 1] * ipiv[ROWS - 1], ipiv[ROWS - 1]
    g88 = g8
    g1_s[ROWS - 1], g8_s[ROWS - 1] = g1, g8
    for y in reversed(range(ROWS - 1)):
        g1 = first[y] * ipiv[y] + ratio[y] * g1
        g8 = ratio[y] * g8
        g1_s[y], g8_s[y] = g1, g8
    for h in range(2):
        for f in range(FIELDS):
            for q, value in enumerate((g1, g88, g8)):
                msg_g[pl.ds(4 * q + 2 * f + h, HALF, stride=16), :] = value[h, :HALF]
        msg_g[pl.ds(12 + h, HALF, stride=16), :] = coef[0][h, :HALF]
        msg_g[pl.ds(14 + h, HALF, stride=16), :] = coef[ROWS - 1][h, :HALF]

    def rows_of(ref, at, count):
        return ref.at[pl.ds(pl.multiple_of(at * count, count), count)]

    def to_solver(msg, got, count, ss, rs, k):
        return pltpu.make_async_remote_copy(
            src_ref=rows_of(msg, k, count), dst_ref=rows_of(got, lat, count),
            send_sem=ss, recv_sem=rs, device_id={"lat": k}, device_id_type=MESH,
        )

    def send_to_solvers(msg, got, count, ss, rs):
        @pl.loop(1, n_lat)
        def _(d):
            k = lax.rem(lat + d, n_lat)

            @pl.when(k < HALF)
            def _():
                to_solver(msg, got, count, ss, rs, k).start()

        @pl.when(solver)
        def _():
            at = pl.ds(pl.multiple_of(lat * count, count), count)
            got[at, :] = msg[at, :]

    def total(ref, rows, ss, rs):
        return pltpu.make_async_remote_copy(
            src_ref=ref.at[pl.ds(0, rows)], dst_ref=ref.at[pl.ds(0, rows)],
            send_sem=ss, recv_sem=rs, device_id={"lat": lax.rem(lat + 1, n_lat)}, device_id_type=MESH,
        )

    send_to_solvers(msg_g, got_g, 16, g_ss, g_rs)

    for t in range(4):
        n = min(ROWS, LEV - ROWS * t)
        coefs = lon_s[0, t, pl.ds(0, n)]
        face_east = jnp.minimum(coefs, roll(coefs, -1))
        face_west = roll(face_east, 1)
        for f in range(FIELDS):
            inner[f, t, pl.ds(0, n)] = diffuse(lon_s[1 + f, t, pl.ds(0, n)], face_east, face_west)

    for halo in halos:
        halo.wait_recv()
    from_west, from_east = halo_in[0], halo_in[1]
    for t in range(4):
        at_west = pick(slot == 1, roll(from_west, 4 - 4 * t), packed[t])
        at_east = pick(slot == 2, roll(from_east, 8 - 4 * t), packed[t])
        done = []
        for side in (at_west, at_east):
            face_east = jnp.minimum(side[0], roll(side[0], -1))
            done.append(diffuse(side[1:], face_east, roll(face_east, 1)))
        both = pick((lane & 15) < 8, done[1], done[0])
        for g in range(min(ROWS, LEV - ROWS * t)):
            whole = pick(
                (lane < 4) | (lane >= 124), roll(both, -16 * g - 8), inner[:, t, g]
            )
            for f in range(FIELDS):
                diff_s[f, pl.ds((ROWS * t + g) * ROWS, ROWS), :] = whole[f]

    for f in range(FIELDS):
        for h in range(2):
            p1 = p8 = jnp.zeros((16, LANES), F32)
            for y in range(ROWS):
                value = by_level(diff_s.at[f], h, y)
                p1 = p1 + g1_s[y, h] * value
                p8 = p8 + g8_s[y, h] * value
            msg_p[pl.ds(2 * f + h, HALF, stride=ROWS), :] = p1[:HALF]
            msg_p[pl.ds(4 + 2 * f + h, HALF, stride=ROWS), :] = p8[:HALF]
    send_to_solvers(msg_p, got_p, ROWS, p_ss, p_rs)

    for f in range(FIELDS):
        for h in range(2):
            values = [by_level(diff_s.at[f], h, y) for y in range(ROWS)]
            for y in range(1, ROWS):
                values[y] = values[y] + ratio_s[y - 1, h] * values[y - 1]
            local = values[ROWS - 1] * ipiv_s[ROWS - 1, h]
            part_s[f, h, ROWS - 1] = local
            for y in reversed(range(ROWS - 1)):
                local = values[y] * ipiv_s[y, h] + ratio_s[y, h] * local
                part_s[f, h, y] = local
    loads[4].wait()
    col = lax.broadcasted_iota(jnp.int32, (32, LANES), 1)
    weights = []
    for f in range(FIELDS):
        vpad[f, 0:LEV, 0:LEV] = vr[:, f, :]
        root = vpad[f]
        root = jnp.where(col < HALF, root, 0.0) + jnp.where((col >= 16) & (col < 28), roll(root, 3), 0.0)
        high = root.astype(BF16)
        low = (root - high.astype(F32)).astype(BF16)
        stacked = jnp.concatenate([high.astype(F32), low.astype(F32)], axis=0)
        weights.append((stacked + roll(stacked, 32)).astype(BF16)[:, :64])

    @pl.when(solver)
    def _():
        total(got_g, (n_lat - 1) * 16, g_ss, g_rs).wait_recv()
        block = [got_g.at[pl.ds(16 * b, 16)] for b in range(n_lat)]
        for m in range(n_lat - 1):
            u = jnp.minimum(block[m][14:16, :], block[m + 1][12:14, :])
            twice_s[m, 0:2] = u
            twice_s[m, 2:4] = u
        gamma = jnp.zeros((4, LANES), F32)
        alphas, betas, gammas = [], [], []
        for m in range(n_lat - 1):
            u = twice_s[m]
            low, up = block[m][8:12, :], block[m + 1][8:12, :]
            own = block[m + 1][0:4, :] + (block[m][4:8, :] - low * gamma)
            beta = u / (1.0 + u * own)
            gamma = beta * up
            alphas.append(beta * low)
            betas.append(beta)
            gammas.append(gamma)
        total(got_p, (n_lat - 1) * ROWS, p_ss, p_rs).wait_recv()
        flux = jnp.zeros((4, LANES), F32)
        reduced = []
        for m in range(n_lat - 1):
            jump = got_p[ROWS * (m + 1) : ROWS * (m + 1) + 4, :] - got_p[ROWS * m + 4 : ROWS * m + 8, :]
            flux = betas[m] * jump + alphas[m] * flux
            reduced.append(flux)
        flux = jnp.zeros((4, LANES), F32)
        msg_f[ROWS * n_lat - 4 : ROWS * n_lat, :] = flux
        msg_f[0:4, :] = flux
        for m in reversed(range(n_lat - 1)):
            flux = reduced[m] + gammas[m] * flux
            msg_f[ROWS * m + 4 : ROWS * m + 8, :] = flux
            msg_f[ROWS * m + 8 : ROWS * m + 12, :] = flux

        @pl.loop(1, n_lat)
        def _(d):
            to_solver(msg_f, got_f, ROWS, f_ss, f_rs, lax.rem(lat + d, n_lat)).start()

        at = pl.ds(pl.multiple_of(lat * ROWS, ROWS), ROWS)
        got_f[at, :] = msg_f[at, :]
        total(got_f, (HALF - 1) * ROWS, f_ss, f_rs).wait_recv()

    @pl.when(jnp.logical_not(solver))
    def _():
        total(got_f, HALF * ROWS, f_ss, f_rs).wait_recv()

    for f in range(FIELDS):
        for h in range(2):
            down = got_f[pl.ds(2 * f + h, 16, stride=ROWS), :]
            up = got_f[pl.ds(4 + 2 * f + h, 16, stride=ROWS), :]
            for y in range(ROWS):
                solved = part_s[f, h, y] + (up * g8_s[y, h] - down * g1_s[y, h])
                high = solved.astype(BF16)
                x_s[f, 16 * h : 16 * h + 16, LANES * y : LANES * (y + 1)] = high
                x_s[f, 32 + 16 * h : 48 + 16 * h, LANES * y : LANES * (y + 1)] = (
                    solved - high.astype(F32)
                ).astype(BF16)
        mixed = jnp.dot(weights[f], x_s[f], preferred_element_type=F32)
        mixed = mixed[0:32] + mixed[32:64]
        for y in range(ROWS):
            rows = pl.ds(y, LEV, stride=ROWS)
            out[f, rows, :] = mixed[0:LEV, LANES * y : LANES * (y + 1)] * ocean_s[rows, :]

    for halo in halos:
        halo.wait_send()

    @pl.when(solver)
    def _():
        total(msg_g, (HALF - 1) * 16, g_ss, g_rs).wait_send()
        total(msg_p, (HALF - 1) * ROWS, p_ss, p_rs).wait_send()
        total(msg_f, (n_lat - 1) * ROWS, f_ss, f_rs).wait_send()

    @pl.when(jnp.logical_not(solver))
    def _():
        total(msg_g, HALF * 16, g_ss, g_rs).wait_send()
        total(msg_p, HALF * ROWS, p_ss, p_rs).wait_send()


def solution(mesh):
    n_lon, n_lat = mesh.shape["lon"], mesh.shape["lat"]

    def per_device(tracer, ocean_mask, kappa_lon, kappa_lat, vertical_root):
        cells = (LEV, ROWS, LANES)
        tiles = (ROWS, 2, 16, LANES)
        made = pl.pallas_call(
            functools.partial(kernel, n_lon, n_lat),
            out_shape=jax.ShapeDtypeStruct((FIELDS, LEV * ROWS, LANES), F32),
            in_specs=[pl.BlockSpec(memory_space=pltpu.HBM)] * 5,
            out_specs=pl.BlockSpec(memory_space=pltpu.VMEM),
            scratch_shapes=[
                pltpu.VMEM((FIELDS,) + cells, F32),
                pltpu.VMEM(cells, jnp.int32),
                pltpu.VMEM(cells, BF16),
                pltpu.VMEM(cells, BF16),
                pltpu.VMEM((LEV, FIELDS, LEV), F32),
                pltpu.VMEM((1 + FIELDS, 4, 8, ROWS, LANES), F32),
                pltpu.VMEM((2, 1 + FIELDS, ROWS, LANES), F32),
                pltpu.VMEM((2, 1 + FIELDS, ROWS, LANES), F32),
                pltpu.VMEM((FIELDS, 4, 8, ROWS, LANES), F32),
                pltpu.VMEM((PAD * ROWS, LANES), F32),
                pltpu.VMEM((FIELDS, PAD * ROWS, LANES), F32),
                pltpu.VMEM((LEV * ROWS, LANES), F32),
                pltpu.VMEM(tiles, F32),
                pltpu.VMEM(tiles, F32),
                pltpu.VMEM(tiles, F32),
                pltpu.VMEM(tiles, F32),
                pltpu.VMEM((FIELDS, 2, ROWS, 16, LANES), F32),
                pltpu.VMEM((HALF * 16, LANES), F32),
                pltpu.VMEM((n_lat * 16, LANES), F32),
                pltpu.VMEM((HALF * ROWS, LANES), F32),
                pltpu.VMEM((n_lat * ROWS, LANES), F32),
                pltpu.VMEM((n_lat * ROWS, LANES), F32),
                pltpu.VMEM((16 * ROWS, LANES), F32),
                pltpu.VMEM((n_lat - 1, 4, LANES), F32),
                pltpu.VMEM((FIELDS, 32, LANES), F32),
                pltpu.VMEM((FIELDS, 64, ROWS * LANES), BF16),
                pltpu.SemaphoreType.DMA((5,)),
                pltpu.SemaphoreType.DMA((2,)),
                pltpu.SemaphoreType.DMA((2,)),
            ]
            + [pltpu.SemaphoreType.DMA] * 6,
            compiler_params=pltpu.CompilerParams(
                collective_id=0, has_side_effects=True, vmem_limit_bytes=60 * 1024 * 1024
            ),
        )(tracer, ocean_mask, kappa_lon, kappa_lat, jnp.moveaxis(vertical_root, 0, 1))
        return made.reshape(FIELDS, LEV, ROWS, LANES)

    placed = (
        P(None, None, "lat", "lon"),
        P(None, "lat", "lon"),
        P(None, "lat", "lon"),
        P(None, "lat", "lon"),
        P(),
    )
    return jax.shard_map(
        per_device,
        mesh=mesh,
        in_specs=placed,
        out_specs=P(None, None, "lat", "lon"),
        check_vma=False,
    )
```

```python
import functools

import jax
import jax.numpy as jnp
from jax import lax
from jax.experimental import pallas as pl
from jax.experimental.pallas import tpu as pltpu
from jax.sharding import PartitionSpec as P

LEV = 25
FIELDS = 2
STEPS = 4
ROWS = 8
LANES = 128
SOLVERS = 2
HALF = 13
PAD = HALF + 16
STARTS = (0, 8, 13, 21)
COUNTS = (8, 5, 8, 4)
MESH = pl.DeviceIdType.MESH
F32 = jnp.float32
BF16 = jnp.bfloat16


def roll(cells, shift):
    return pltpu.roll(cells, shift % LANES, axis=cells.ndim - 1)


def pick(mask, yes, no):
    return jnp.where(jnp.broadcast_to(mask, yes.shape), yes, no)


def by_level(ref, row):
    return jnp.stack(
        [ref[pl.ds(half * HALF * ROWS + row, 16, stride=ROWS), :] for half in range(2)]
    )


def by_row(ref, row):
    return ref[pl.ds(row, ROWS, stride=ROWS), :]


def diffuse(state, face_east, face_west):
    for _ in range(STEPS):
        state = state + (
            face_east * (roll(state, -1) - state) - face_west * (state - roll(state, 1))
        )
    return state


def factor(coef):
    ones = jnp.ones_like(coef[0])
    excess = jnp.zeros_like(ones)
    ratio, ipiv, first = [], [], [ones]
    for y in range(ROWS - 1):
        face = jnp.minimum(coef[y], coef[y + 1])
        ipiv.append(1.0 / (1.0 + face + excess))
        ratio.append(face * ipiv[y])
        excess = ratio[y] * (1.0 + excess)
        first.append(ratio[y] * first[y])
    ipiv.append(1.0 / (1.0 + excess))
    g1, g8 = [first[-1] * ipiv[-1]], [ipiv[-1]]
    for y in reversed(range(ROWS - 1)):
        g1.append(first[y] * ipiv[y] + ratio[y] * g1[-1])
        g8.append(ratio[y] * g8[-1])
    return ratio, ipiv, g1[::-1], g8[::-1]


def kernel(
    n_lon, n_lat,
    tr_h, mk_h, kl_h, kt_h, vr_h, out,
    tr, mk, kl, kt, vr,
    lon_s, halo_out, halo_in, lat_s, diff_s, ocean_s,
    ratio_s, ipiv_s, g1_s, g8_s, part_s, edge_c, edge_s, edge_g1, edge_g8,
    msg_g, got_g, msg_p, got_p, msg_f, got_f,
    msg_ge, got_ge, msg_pe, got_pe, msg_fe, got_fe,
    line_s, line_e, flux_s, vpad, x_s,
    in_sem, halo_ss, halo_rs, g_ss, g_rs, p_ss, p_rs, f_ss, f_rs, e_ss, e_rs,
):
    lon, lat = lax.axis_index("lon"), lax.axis_index("lat")
    east, west = lax.rem(lon + 1, n_lon), lax.rem(lon + n_lon - 1, n_lon)
    solver = lat < SOLVERS

    loads = [
        pltpu.make_async_copy(src, dst, in_sem.at[i])
        for i, (src, dst) in enumerate(
            ((mk_h, mk), (kl_h, kl), (tr_h, tr), (kt_h, kt), (vr_h, vr))
        )
    ]
    for load in loads:
        load.start()

    barrier = pltpu.get_barrier_semaphore()
    pl.semaphore_signal(barrier, inc=1, device_id={"lon": west}, device_id_type=MESH)

    @pl.when(solver)
    def _():
        @pl.loop(1, n_lat)
        def _(d):
            pl.semaphore_signal(
                barrier, inc=1, device_id={"lat": lax.rem(lat + d, n_lat)}, device_id_type=MESH
            )

    lane = lax.broadcasted_iota(jnp.int32, (ROWS, LANES), 1)
    slot = (lane >> 2) & 3
    group = lane >> 4
    edge = (lane < 4) | (lane >= LANES - 4)

    flux_s[...] = jnp.zeros(flux_s.shape, F32)
    vpad[...] = jnp.zeros(vpad.shape, F32)
    spare = pl.ds(LEV * ROWS, (PAD - LEV) * ROWS)
    lat_s[spare, :] = jnp.zeros(((PAD - LEV) * ROWS, LANES), F32)
    for f in range(FIELDS):
        diff_s[f, spare, :] = jnp.zeros(((PAD - LEV) * ROWS, LANES), F32)

    loads[0].wait()
    loads[1].wait()
    loads[2].wait()
    packed = []
    for t in range(4):
        n = COUNTS[t]
        levels = pl.ds(STARTS[t], n)
        ocean = mk[levels].astype(F32)
        ocean_s[pl.ds(STARTS[t] * ROWS, n * ROWS), :] = ocean.reshape(n * ROWS, LANES)
        lon_s[0, t, pl.ds(0, n)] = kl[levels].astype(F32) * ocean
        for f in range(FIELDS):
            lon_s[1 + f, t, pl.ds(0, n)] = tr[f, levels] * ocean
        tile = roll(lon_s[:, t, 0], 8)
        for g in range(1, n):
            tile = pick(group == 8 - g, roll(lon_s[:, t, g], 8 - 16 * g), tile)
        packed.append(tile)
    to_east, to_west = roll(packed[0], -4), roll(packed[0], -8)
    for t in range(1, 4):
        to_east = pick(slot == t, roll(packed[t], 4 * t - 4), to_east)
        to_west = pick(slot == t, roll(packed[t], 4 * t - 8), to_west)
    halo_out[0] = to_east
    halo_out[1] = to_west
    halos = [
        pltpu.make_async_remote_copy(
            src_ref=halo_out.at[i], dst_ref=halo_in.at[i],
            send_sem=halo_ss.at[i], recv_sem=halo_rs.at[i],
            device_id={"lon": side}, device_id_type=MESH,
        )
        for i, side in enumerate((east, west))
    ]

    @pl.when(solver)
    def _():
        pl.semaphore_wait(barrier, SOLVERS)

    @pl.when(jnp.logical_not(solver))
    def _():
        pl.semaphore_wait(barrier, SOLVERS + 1)

    halos[0].start()

    def to_solver(msg, got, h, ss, rs):
        return pltpu.make_async_remote_copy(
            src_ref=msg, dst_ref=got.at[lat], send_sem=ss.at[h], recv_sem=rs.at[h],
            device_id={"lat": h}, device_id_type=MESH,
        )

    def of_solver(msg, got, h, k, ss, rs):
        return pltpu.make_async_remote_copy(
            src_ref=msg.at[k], dst_ref=got, send_sem=ss.at[h], recv_sem=rs.at[h],
            device_id={"lat": k}, device_id_type=MESH,
        )

    def send(h, msg, got, ss, rs):
        @pl.when(lat != h)
        def _():
            to_solver(msg, got, h, ss, rs).start()

        @pl.when(lat == h)
        def _():
            got[lat] = msg[...]

    loads[3].wait()
    lat_s[pl.ds(0, LEV * ROWS), :] = kt[...].astype(F32).reshape(LEV * ROWS, LANES) * ocean_s[...]
    coef = [by_level(lat_s, y) for y in range(ROWS)]
    ratio, ipiv, g1, g8 = factor(coef)
    for y in range(ROWS):
        ipiv_s[y], g1_s[y], g8_s[y] = ipiv[y], g1[y], g8[y]
        if y < ROWS - 1:
            ratio_s[y] = ratio[y]
    for h in range(SOLVERS):
        for q, value in enumerate((g1[0], g8[-1], g8[0], coef[0], coef[-1])):
            msg_g[h, q] = value[h, :HALF]
    for t in range(4):
        tile = roll(lat_s[pl.ds(STARTS[t] * ROWS, ROWS), :], 8)
        for g in range(1, COUNTS[t]):
            tile = pick(
                group == 8 - g, roll(lat_s[pl.ds((STARTS[t] + g) * ROWS, ROWS), :], 8 - 16 * g), tile
            )
        for f in range(FIELDS):
            edge_c[pl.ds((4 * f + t) * ROWS, ROWS), :] = tile
    coef = [by_row(edge_c, y) for y in range(ROWS)]
    unused, unused, g1, g8 = factor(coef)
    for y in range(ROWS):
        edge_g1[y], edge_g8[y] = g1[y], g8[y]
    for q, value in enumerate((g1[0], g8[-1], g8[0], coef[0], coef[-1])):
        msg_ge[q] = value[0:4]
    for h in range(SOLVERS):
        send(h, msg_g.at[h], got_g, g_ss, g_rs)
    send(1, msg_ge, got_ge, e_ss.at[0], e_rs.at[0])

    halos[0].wait_recv()
    halos[1].start()

    for t in range(4):
        n = COUNTS[t]
        coefs = lon_s[0, t, pl.ds(0, n)]
        face_east = jnp.minimum(coefs, roll(coefs, -1))
        face_west = roll(face_east, 1)
        for f in range(FIELDS):
            diff_s[f, pl.ds(STARTS[t] * ROWS, n * ROWS), :] = diffuse(
                lon_s[1 + f, t, pl.ds(0, n)], face_east, face_west
            ).reshape(n * ROWS, LANES)
    for f in range(FIELDS):
        p1 = p8 = jnp.zeros((2, 16, LANES), F32)
        for y in range(ROWS):
            value = by_level(diff_s.at[f], y)
            p1 = p1 + g1_s[y] * value
            p8 = p8 + g8_s[y] * value
        for h in range(SOLVERS):
            msg_p[h, 2 * f] = p1[h, :HALF]
            msg_p[h, 2 * f + 1] = p8[h, :HALF]
    for h in range(SOLVERS):
        send(h, msg_p.at[h], got_p, p_ss, p_rs)

    halos[1].wait_recv()
    from_west, from_east = halo_in[0], halo_in[1]
    edges = []
    for t in range(4):
        at_west = pick(slot == 1, roll(from_west, 4 - 4 * t), packed[t])
        at_east = pick(slot == 2, roll(from_east, 8 - 4 * t), packed[t])
        done = []
        for side in (at_west, at_east):
            face_east = jnp.minimum(side[0], roll(side[0], -1))
            done.append(diffuse(side[1:], face_east, roll(face_east, 1)))
        edges.append(pick((lane & 15) < 8, done[1], done[0]))
        for f in range(FIELDS):
            edge_s[pl.ds((4 * f + t) * ROWS, ROWS), :] = edges[t][f]
    p1 = p8 = jnp.zeros((ROWS, LANES), F32)
    for y in range(ROWS):
        value = by_row(edge_s, y)
        p1 = p1 + edge_g1[y] * value
        p8 = p8 + edge_g8[y] * value
    msg_pe[0] = p1
    msg_pe[1] = p8
    send(1, msg_pe, got_pe, e_ss.at[1], e_rs.at[1])

    for t in range(4):
        for g in range(COUNTS[t]):
            rows = pl.ds((STARTS[t] + g) * ROWS, ROWS)
            ends = roll(edges[t], 16 * g - 8)
            for f in range(FIELDS):
                diff_s[f, rows, :] = jnp.where(edge, ends[f], diff_s[f, rows, :])
    for f in range(FIELDS):
        values = [by_level(diff_s.at[f], y) for y in range(ROWS)]
        for y in range(1, ROWS):
            values[y] = values[y] + ratio_s[y - 1] * values[y - 1]
        local = values[ROWS - 1] * ipiv_s[ROWS - 1]
        part_s[f, ROWS - 1] = local
        for y in reversed(range(ROWS - 1)):
            local = values[y] * ipiv_s[y] + ratio_s[y] * local
            part_s[f, y] = local
    loads[4].wait()
    col = lax.broadcasted_iota(jnp.int32, (32, LANES), 1)
    weights = []
    for f in range(FIELDS):
        vpad[f, 0:LEV, 0:LEV] = vr[:, f, :]
        root = vpad[f]
        root = jnp.where(col < HALF, root, 0.0) + jnp.where(
            (col >= 16) & (col < 16 + LEV - HALF), roll(root, 16 - HALF), 0.0
        )
        high = root.astype(BF16).astype(F32)
        stacked = jnp.concatenate([high, root - high], axis=0)
        weights.append((stacked + roll(stacked, 32)).astype(BF16)[:, :64])

    def total(ref, ss, rs):
        return pltpu.make_async_remote_copy(
            src_ref=ref, dst_ref=ref, send_sem=ss, recv_sem=rs,
            device_id={"lat": lax.rem(lat + 1, n_lat)}, device_id_type=MESH,
        )

    others = pl.ds(0, n_lat - 1)

    def lines(block, shape, keep):
        gamma = jnp.zeros(shape, F32)
        for m in range(n_lat - 1):
            u = jnp.minimum(block(m, 4), block(m + 1, 3))
            low = block(m, 2)
            own = block(m + 1, 0) + (block(m, 1) - low * gamma)
            beta = u / (1.0 + u * own)
            gamma = beta * block(m + 1, 2)
            for q, value in enumerate((beta, beta * low, gamma)):
                keep[m, q] = value

    def fluxes(jump, line, shape, put):
        flux = jnp.zeros(shape, F32)
        reduced = []
        for m in range(n_lat - 1):
            flux = line(m, 0) * jump(m) + line(m, 1) * flux
            reduced.append(flux)
        flux = jnp.zeros(shape, F32)
        put(n_lat - 1, 1, flux)
        put(0, 0, flux)
        for m in reversed(range(n_lat - 1)):
            flux = reduced[m] + line(m, 2) * flux
            put(m, 1, flux)
            put(m + 1, 0, flux)

    for h in range(SOLVERS):

        @pl.when(lat == h)
        def _():
            total(got_g.at[others], g_ss.at[h], g_rs.at[h]).wait_recv()
            lines(lambda b, q: got_g[b, q], (HALF, LANES), line_s)
            if h == 1:
                total(got_ge.at[others], e_ss.at[0, h], e_rs.at[0, h]).wait_recv()
                for e in range(2):
                    lines(lambda b, q: got_ge[b, q], (4, LANES), line_e.at[:, :, pl.ds(4 * e, 4)])
            total(got_p.at[others], p_ss.at[h], p_rs.at[h]).wait_recv()
            for f in range(FIELDS):

                def put(b, end, flux):
                    msg_f[b, 2 * f + end] = flux

                fluxes(
                    lambda m: got_p[m + 1, 2 * f] - got_p[m, 2 * f + 1],
                    lambda m, q: line_s[m, q], (HALF, LANES), put,
                )

            @pl.loop(1, n_lat)
            def _(d):
                of_solver(msg_f, got_f.at[h], h, lax.rem(lat + d, n_lat), f_ss, f_rs).start()

            got_f[h] = msg_f[h]

    for h in range(SOLVERS):

        @pl.when(lat != h)
        def _():
            of_solver(msg_f, got_f.at[h], h, h, f_ss, f_rs).wait_recv()

        flux_s[h, :, 0:HALF] = got_f[h]

    @pl.when(lat == 1)
    def _():
        total(got_pe.at[others], e_ss.at[1, 1], e_rs.at[1, 1]).wait_recv()

        def put(b, end, flux):
            msg_fe[b, end] = flux

        fluxes(
            lambda m: got_pe[m + 1, 0] - got_pe[m, 1],
            lambda m, q: line_e[m, q], (ROWS, LANES), put,
        )

        @pl.loop(1, n_lat)
        def _(d):
            of_solver(msg_fe, got_fe, 1, lax.rem(lat + d, n_lat), e_ss.at[2], e_rs.at[2]).start()

        got_fe[...] = msg_fe[1]

    @pl.when(lat != 1)
    def _():
        of_solver(msg_fe, got_fe, 1, 1, e_ss.at[2], e_rs.at[2]).wait_recv()

    flux_e = roll(got_fe[...], -8)
    for f in range(FIELDS):
        for h in range(2):
            flux = []
            for end in range(2):
                tiles = []
                for a in range(2):
                    row = 4 * f + 2 * h + a
                    ends = pltpu.roll(
                        jnp.broadcast_to(flux_e[end, row : row + 1], (ROWS, LANES)),
                        0, axis=1, stride=16, stride_axis=0,
                    )
                    tiles.append(
                        jnp.where(edge, ends, flux_s[h, 2 * f + end, ROWS * a : ROWS * (a + 1)])
                    )
                flux.append(jnp.concatenate(tiles, axis=0))
            for y in range(ROWS):
                solved = part_s[f, y, h] + (flux[1] * g8_s[y, h] - flux[0] * g1_s[y, h])
                high = solved.astype(BF16)
                x_s[f, 16 * h : 16 * h + 16, LANES * y : LANES * (y + 1)] = high
                x_s[f, 32 + 16 * h : 48 + 16 * h, LANES * y : LANES * (y + 1)] = (
                    solved - high.astype(F32)
                ).astype(BF16)
        mixed = jnp.dot(weights[f], x_s[f], preferred_element_type=F32)
        mixed = mixed[0:32] + mixed[32:64]
        for y in range(ROWS):
            rows = pl.ds(y, LEV, stride=ROWS)
            out[f, rows, :] = mixed[0:LEV, LANES * y : LANES * (y + 1)] * ocean_s[rows, :]

    for halo in halos:
        halo.wait_send()
    for h in range(SOLVERS):

        @pl.when(lat != h)
        def _():
            to_solver(msg_g.at[h], got_g, h, g_ss, g_rs).wait_send()
            to_solver(msg_p.at[h], got_p, h, p_ss, p_rs).wait_send()
            if h == 1:
                to_solver(msg_ge, got_ge, h, e_ss.at[0], e_rs.at[0]).wait_send()
                to_solver(msg_pe, got_pe, h, e_ss.at[1], e_rs.at[1]).wait_send()

        @pl.when(lat == h)
        def _():
            total(msg_f.at[others], f_ss.at[h], f_rs.at[h]).wait_send()
            if h == 1:
                total(msg_fe.at[others], e_ss.at[2, h], e_rs.at[2, h]).wait_send()


def solution(mesh):
    n_lon, n_lat = mesh.shape["lon"], mesh.shape["lat"]

    def per_device(tracer, ocean_mask, kappa_lon, kappa_lat, vertical_root):
        cells = (LEV, ROWS, LANES)
        natural = (PAD * ROWS, LANES)
        rows = (ROWS, 2, 16, LANES)
        scratch = [
            (FIELDS,) + cells,
            (cells, jnp.int32),
            (cells, BF16),
            (cells, BF16),
            (LEV, FIELDS, LEV),
            (1 + FIELDS, 4, 8, ROWS, LANES),
            (2, 1 + FIELDS, ROWS, LANES),
            (2, 1 + FIELDS, ROWS, LANES),
            natural,
            (FIELDS,) + natural,
            (LEV * ROWS, LANES),
            rows, rows, rows, rows,
            (FIELDS,) + rows,
            (64, LANES), (64, LANES),
            (ROWS, ROWS, LANES), (ROWS, ROWS, LANES),
            (SOLVERS, 5, HALF, LANES), (n_lat, 5, HALF, LANES),
            (SOLVERS, 4, HALF, LANES), (n_lat, 4, HALF, LANES),
            (n_lat, 4, HALF, LANES), (SOLVERS, 4, HALF, LANES),
            (5, 4, LANES), (n_lat, 5, 4, LANES),
            (2, ROWS, LANES), (n_lat, 2, ROWS, LANES),
            (n_lat, 2, ROWS, LANES), (2, ROWS, LANES),
            (n_lat - 1, 3, HALF, LANES),
            (n_lat - 1, 3, ROWS, LANES),
            (SOLVERS, 4, 16, LANES),
            (FIELDS, 32, LANES),
            ((FIELDS, 64, ROWS * LANES), BF16),
        ]
        scratch = [
            pltpu.VMEM(*item) if isinstance(item[0], tuple) else pltpu.VMEM(item, F32)
            for item in scratch
        ]
        sems = [(5,), (2,), (2,)] + [(SOLVERS,)] * 6 + [(3, SOLVERS)] * 2
        made = pl.pallas_call(
            functools.partial(kernel, n_lon, n_lat),
            out_shape=pltpu.VMEM((FIELDS, LEV * ROWS, LANES), F32),
            in_specs=[pl.BlockSpec(memory_space=pltpu.HBM)] * 5,
            out_specs=pl.BlockSpec(memory_space=pltpu.VMEM),
            scratch_shapes=scratch + [pltpu.SemaphoreType.DMA(shape) for shape in sems],
            compiler_params=pltpu.CompilerParams(
                collective_id=0, has_side_effects=True, vmem_limit_bytes=60 * 1024 * 1024
            ),
        )(tracer, ocean_mask, kappa_lon, kappa_lat, jnp.moveaxis(vertical_root, 0, 1))
        return made.reshape(FIELDS, LEV, ROWS, LANES)

    placed = (
        P(None, None, "lat", "lon"),
        P(None, "lat", "lon"),
        P(None, "lat", "lon"),
        P(None, "lat", "lon"),
        P(),
    )
    return jax.shard_map(
        per_device,
        mesh=mesh,
        in_specs=placed,
        out_specs=P(None, None, "lat", "lon"),
        check_vma=False,
    )
```

```python
import functools

import jax
import jax.numpy as jnp
from jax import lax
from jax.experimental import pallas as pl
from jax.experimental.pallas import tpu as pltpu
from jax.sharding import PartitionSpec as P

LEV = 25
FIELDS = 2
STEPS = 4
ROWS = 8
LANES = 128
HALF = 13
ENDS = 1
PAD = HALF + 16
STARTS = (0, 8, 13, 21)
COUNTS = (8, 5, 8, 4)
MESH = pl.DeviceIdType.MESH
F32 = jnp.float32
BF16 = jnp.bfloat16


def roll(cells, shift):
    return pltpu.roll(cells, shift % LANES, axis=cells.ndim - 1)


def pick(mask, yes, no):
    return jnp.where(jnp.broadcast_to(mask, yes.shape), yes, no)


def by_level(ref, row):
    return jnp.stack(
        [ref[pl.ds(half * HALF * ROWS + row, 16, stride=ROWS), :] for half in range(2)]
    )


def by_row(ref, row):
    return ref[pl.ds(row, ROWS, stride=ROWS), :]


def diffuse(state, face_east, face_west):
    for _ in range(STEPS):
        state = state + (
            face_east * (roll(state, -1) - state) - face_west * (state - roll(state, 1))
        )
    return state


def factor(coef):
    ones = jnp.ones_like(coef[0])
    excess = jnp.zeros_like(ones)
    ratio, ipiv, first = [], [], [ones]
    for y in range(ROWS - 1):
        face = jnp.minimum(coef[y], coef[y + 1])
        ipiv.append(1.0 / (1.0 + face + excess))
        ratio.append(face * ipiv[y])
        excess = ratio[y] * (1.0 + excess)
        first.append(ratio[y] * first[y])
    ipiv.append(1.0 / (1.0 + excess))
    g1, g8 = [first[-1] * ipiv[-1]], [ipiv[-1]]
    for y in reversed(range(ROWS - 1)):
        g1.append(first[y] * ipiv[y] + ratio[y] * g1[-1])
        g8.append(ratio[y] * g8[-1])
    return ratio, ipiv, g1[::-1], g8[::-1]


def kernel(
    n_lon, n_lat,
    tr_h, mk_h, kl_h, kt_h, vr_h, out,
    tr, mk, kl, kt, vr,
    lon_s, halo_out, halo_in, lat_s, diff_s, ocean_s,
    ratio_s, ipiv_s, g1_s, g8_s, part_s, edge_c, edge_s, edge_g1, edge_g8,
    msg_g, got_g, msg_p, got_p, msg_f, got_f,
    msg_ge, got_ge, msg_pe, got_pe, msg_fe, got_fe,
    line_s, line_e, vpad, x_s,
    in_sem, halo_ss, halo_rs, g_ss, g_rs, p_ss, p_rs, f_ss, f_rs, e_ss, e_rs,
):
    lon, lat = lax.axis_index("lon"), lax.axis_index("lat")
    east, west = lax.rem(lon + 1, n_lon), lax.rem(lon + n_lon - 1, n_lon)
    solver = lat < HALF

    loads = [
        pltpu.make_async_copy(src, dst, in_sem.at[i])
        for i, (src, dst) in enumerate(
            ((mk_h, mk), (kl_h, kl), (tr_h, tr), (kt_h, kt), (vr_h, vr))
        )
    ]
    for load in loads:
        load.start()

    barrier = pltpu.get_barrier_semaphore()
    for side in (east, west):
        pl.semaphore_signal(barrier, inc=1, device_id={"lon": side}, device_id_type=MESH)

    @pl.when(solver)
    def _():
        @pl.loop(1, n_lat)
        def _(d):
            pl.semaphore_signal(
                barrier, inc=1, device_id={"lat": lax.rem(lat + d, n_lat)}, device_id_type=MESH
            )

    lane = lax.broadcasted_iota(jnp.int32, (ROWS, LANES), 1)
    slot = (lane >> 2) & 3
    group = lane >> 4
    edge = (lane < 4) | (lane >= LANES - 4)

    got_f[HALF:16] = jnp.zeros((16 - HALF, ROWS, LANES), F32)
    vpad[...] = jnp.zeros(vpad.shape, F32)
    spare = pl.ds(LEV * ROWS, (PAD - LEV) * ROWS)
    lat_s[spare, :] = jnp.zeros(((PAD - LEV) * ROWS, LANES), F32)
    for f in range(FIELDS):
        diff_s[f, spare, :] = jnp.zeros(((PAD - LEV) * ROWS, LANES), F32)

    loads[0].wait()
    loads[1].wait()
    loads[2].wait()
    packed = []
    for t in range(4):
        n = COUNTS[t]
        levels = pl.ds(STARTS[t], n)
        ocean = mk[levels].astype(F32)
        ocean_s[pl.ds(STARTS[t] * ROWS, n * ROWS), :] = ocean.reshape(n * ROWS, LANES)
        lon_s[0, t, pl.ds(0, n)] = kl[levels].astype(F32) * ocean
        for f in range(FIELDS):
            lon_s[1 + f, t, pl.ds(0, n)] = tr[f, levels] * ocean
        tile = roll(lon_s[:, t, 0], 8)
        for g in range(1, n):
            tile = pick(group == 8 - g, roll(lon_s[:, t, g], 8 - 16 * g), tile)
        packed.append(tile)
    to_east, to_west = roll(packed[0], -4), roll(packed[0], -8)
    for t in range(1, 4):
        to_east = pick(slot == t, roll(packed[t], 4 * t - 4), to_east)
        to_west = pick(slot == t, roll(packed[t], 4 * t - 8), to_west)
    halo_out[0] = to_east
    halo_out[1] = to_west
    halos = [
        pltpu.make_async_remote_copy(
            src_ref=halo_out.at[i], dst_ref=halo_in.at[i],
            send_sem=halo_ss.at[i], recv_sem=halo_rs.at[i],
            device_id={"lon": side}, device_id_type=MESH,
        )
        for i, side in enumerate((east, west))
    ]

    @pl.when(solver)
    def _():
        pl.semaphore_wait(barrier, HALF + 1)

    @pl.when(jnp.logical_not(solver))
    def _():
        pl.semaphore_wait(barrier, HALF + 2)

    for halo in halos:
        halo.start()

    def tile_to(msg, got, ss, rs, k):
        return pltpu.make_async_remote_copy(
            src_ref=msg.at[k], dst_ref=got.at[lat],
            send_sem=ss, recv_sem=rs, device_id={"lat": k}, device_id_type=MESH,
        )

    def send_to_solvers(msg, got, ss, rs):
        @pl.loop(1, n_lat)
        def _(d):
            k = lax.rem(lat + d, n_lat)

            @pl.when(k < HALF)
            def _():
                tile_to(msg, got, ss, rs, k).start()

        @pl.when(solver)
        def _():
            got[lat] = msg[lat]

    def total(ref, ss, rs):
        return pltpu.make_async_remote_copy(
            src_ref=ref, dst_ref=ref, send_sem=ss, recv_sem=rs,
            device_id={"lat": lax.rem(lat + 1, n_lat)}, device_id_type=MESH,
        )

    def to_ends(msg, got, i):
        return pltpu.make_async_remote_copy(
            src_ref=msg, dst_ref=got.at[lat], send_sem=e_ss.at[i], recv_sem=e_rs.at[i],
            device_id={"lat": ENDS}, device_id_type=MESH,
        )

    def of_ends(k):
        return pltpu.make_async_remote_copy(
            src_ref=msg_fe.at[k], dst_ref=got_fe, send_sem=e_ss.at[2], recv_sem=e_rs.at[2],
            device_id={"lat": k}, device_id_type=MESH,
        )

    def send_to_ends(msg, got, i):
        @pl.when(lat != ENDS)
        def _():
            to_ends(msg, got, i).start()

        @pl.when(lat == ENDS)
        def _():
            got[ENDS] = msg[...]

    loads[3].wait()
    lat_s[pl.ds(0, LEV * ROWS), :] = kt[...].astype(F32).reshape(LEV * ROWS, LANES) * ocean_s[...]
    coef = [by_level(lat_s, y) for y in range(ROWS)]
    ratio, ipiv, g1, g8 = factor(coef)
    for y in range(ROWS):
        ipiv_s[y], g1_s[y], g8_s[y] = ipiv[y], g1[y], g8[y]
        if y < ROWS - 1:
            ratio_s[y] = ratio[y]
    for h in range(2):
        for q, value in enumerate((g1[0], g8[-1], g8[0], coef[0], coef[-1])):
            msg_g[:, 2 * q + h, :] = value[h, :HALF]
    send_to_solvers(msg_g, got_g, g_ss, g_rs)
    for t in range(4):
        tile = roll(lat_s[pl.ds(STARTS[t] * ROWS, ROWS), :], 8)
        for g in range(1, COUNTS[t]):
            tile = pick(
                group == 8 - g, roll(lat_s[pl.ds((STARTS[t] + g) * ROWS, ROWS), :], 8 - 16 * g), tile
            )
        for f in range(FIELDS):
            edge_c[pl.ds((4 * f + t) * ROWS, ROWS), :] = tile
    coef = [by_row(edge_c, y) for y in range(ROWS)]
    unused, unused, g1, g8 = factor(coef)
    for y in range(ROWS):
        edge_g1[y], edge_g8[y] = g1[y], g8[y]
    for q, value in enumerate((g1[0], g8[-1], g8[0], coef[0], coef[-1])):
        msg_ge[q] = value[0:4]
    send_to_ends(msg_ge, got_ge, 0)

    for t in range(4):
        n = COUNTS[t]
        coefs = lon_s[0, t, pl.ds(0, n)]
        face_east = jnp.minimum(coefs, roll(coefs, -1))
        face_west = roll(face_east, 1)
        for f in range(FIELDS):
            diff_s[f, pl.ds(STARTS[t] * ROWS, n * ROWS), :] = diffuse(
                lon_s[1 + f, t, pl.ds(0, n)], face_east, face_west
            ).reshape(n * ROWS, LANES)
    for f in range(FIELDS):
        p1 = p8 = jnp.zeros((2, 16, LANES), F32)
        for y in range(ROWS):
            value = by_level(diff_s.at[f], y)
            p1 = p1 + g1_s[y] * value
            p8 = p8 + g8_s[y] * value
        for h in range(2):
            msg_p[:, 2 * f + h, :] = p1[h, :HALF]
            msg_p[:, 4 + 2 * f + h, :] = p8[h, :HALF]
    send_to_solvers(msg_p, got_p, p_ss, p_rs)

    others = n_lat - 1

    def lines(face, own_first, own_last, cross, shape, keep):
        gamma = jnp.zeros(shape, F32)
        for m in range(others):
            low = cross(m)
            beta = face(m)
            beta = beta / (1.0 + beta * (own_first(m + 1) + (own_last(m) - low * gamma)))
            gamma = beta * cross(m + 1)
            for q, value in enumerate((beta, beta * low, gamma)):
                for ref in keep:
                    ref[m, q] = value

    def fluxes(jump, line, shape, put):
        flux = jnp.zeros(shape, F32)
        reduced = []
        for m in range(others):
            flux = line[m, 0] * jump(m) + line[m, 1] * flux
            reduced.append(flux)
        flux = jnp.zeros(shape, F32)
        put(others, 1, flux)
        put(0, 0, flux)
        for m in reversed(range(others)):
            flux = reduced[m] + line[m, 2] * flux
            put(m, 1, flux)
            put(m + 1, 0, flux)

    for halo in halos:
        halo.wait_recv()
    from_west, from_east = halo_in[0], halo_in[1]
    edges = []
    for t in range(4):
        at_west = pick(slot == 1, roll(from_west, 4 - 4 * t), packed[t])
        at_east = pick(slot == 2, roll(from_east, 8 - 4 * t), packed[t])
        done = []
        for side in (at_west, at_east):
            face_east = jnp.minimum(side[0], roll(side[0], -1))
            done.append(diffuse(side[1:], face_east, roll(face_east, 1)))
        edges.append(pick((lane & 15) < 8, done[1], done[0]))
        for f in range(FIELDS):
            edge_s[pl.ds((4 * f + t) * ROWS, ROWS), :] = edges[t][f]
    p1 = p8 = jnp.zeros((ROWS, LANES), F32)
    for y in range(ROWS):
        value = by_row(edge_s, y)
        p1 = p1 + edge_g1[y] * value
        p8 = p8 + edge_g8[y] * value
    msg_pe[0] = p1
    msg_pe[1] = p8
    send_to_ends(msg_pe, got_pe, 1)

    @pl.when(solver)
    def _():
        total(got_g.at[pl.ds(0, others)], g_ss, g_rs).wait_recv()

        def part(q):
            return lambda b: got_g[b, 2 * q : 2 * q + 2, :]

        lines(
            lambda m: jnp.minimum(part(4)(m), part(3)(m + 1)), part(0), part(1), part(2),
            (2, LANES), [line_s.at[:, :, pl.ds(2 * f, 2)] for f in range(FIELDS)],
        )
        total(got_p.at[pl.ds(0, others)], p_ss, p_rs).wait_recv()

        def put(b, end, flux):
            msg_f[b, 4 * end : 4 * end + 4, :] = flux

        fluxes(
            lambda m: got_p[m + 1, 0:4, :] - got_p[m, 4:8, :], line_s, (4, LANES), put
        )

        @pl.loop(0, n_lat)
        def _(k):
            @pl.when(k != lat)
            def _():
                tile_to(msg_f, got_f, f_ss, f_rs, k).start()

        got_f[lat] = msg_f[lat]


    for t in range(4):
        for g in range(COUNTS[t]):
            rows = pl.ds((STARTS[t] + g) * ROWS, ROWS)
            ends = roll(edges[t], 16 * g - 8)
            for f in range(FIELDS):
                diff_s[f, rows, :] = jnp.where(edge, ends[f], diff_s[f, rows, :])
    for f in range(FIELDS):
        values = [by_level(diff_s.at[f], y) for y in range(ROWS)]
        for y in range(1, ROWS):
            values[y] = values[y] + ratio_s[y - 1] * values[y - 1]
        local = values[ROWS - 1] * ipiv_s[ROWS - 1]
        part_s[f, ROWS - 1] = local
        for y in reversed(range(ROWS - 1)):
            local = values[y] * ipiv_s[y] + ratio_s[y] * local
            part_s[f, y] = local
    loads[4].wait()
    col = lax.broadcasted_iota(jnp.int32, (32, LANES), 1)
    weights = []
    for f in range(FIELDS):
        vpad[f, 0:LEV, 0:LEV] = vr[:, f, :]
        root = vpad[f]
        root = jnp.where(col < HALF, root, 0.0) + jnp.where(
            (col >= 16) & (col < 16 + LEV - HALF), roll(root, 16 - HALF), 0.0
        )
        high = root.astype(BF16).astype(F32)
        stacked = jnp.concatenate([high, root - high], axis=0)
        weights.append((stacked + roll(stacked, 32)).astype(BF16)[:, :64])

    @pl.when(lat == ENDS)
    def _():
        total(got_ge.at[pl.ds(0, others)], e_ss.at[0], e_rs.at[0]).wait_recv()
        lines(
            lambda m: jnp.minimum(got_ge[m, 4], got_ge[m + 1, 3]),
            lambda b: got_ge[b, 0], lambda b: got_ge[b, 1], lambda b: got_ge[b, 2],
            (4, LANES), [line_e.at[:, :, pl.ds(4 * f, 4)] for f in range(FIELDS)],
        )
        total(got_pe.at[pl.ds(0, others)], e_ss.at[1], e_rs.at[1]).wait_recv()

        def put(b, end, flux):
            msg_fe[b, end] = flux

        fluxes(lambda m: got_pe[m + 1, 0] - got_pe[m, 1], line_e, (ROWS, LANES), put)

        @pl.loop(1, n_lat)
        def _(d):
            of_ends(lax.rem(lat + d, n_lat)).start()

        got_fe[...] = msg_fe[ENDS]

    @pl.when(solver)
    def _():
        total(got_f.at[pl.ds(0, HALF - 1)], f_ss, f_rs).wait_recv()

    @pl.when(jnp.logical_not(solver))
    def _():
        total(got_f.at[pl.ds(0, HALF)], f_ss, f_rs).wait_recv()

    @pl.when(lat != ENDS)
    def _():
        of_ends(ENDS).wait_recv()

    flux_e = roll(got_fe[...], -8)
    for f in range(FIELDS):
        for h in range(2):
            flux = []
            for end in range(2):
                inside = got_f[:, 4 * end + 2 * f + h, :]
                tiles = []
                for a in range(2):
                    row = 4 * f + 2 * h + a
                    ends = pltpu.roll(
                        jnp.broadcast_to(flux_e[end, row : row + 1], (ROWS, LANES)),
                        0, axis=1, stride=16, stride_axis=0,
                    )
                    tiles.append(
                        jnp.where(edge, ends, inside[ROWS * a : ROWS * (a + 1)])
                    )
                flux.append(jnp.concatenate(tiles, axis=0))
            for y in range(ROWS):
                solved = part_s[f, y, h] + (flux[1] * g8_s[y, h] - flux[0] * g1_s[y, h])
                high = solved.astype(BF16)
                x_s[f, 16 * h : 16 * h + 16, LANES * y : LANES * (y + 1)] = high
                x_s[f, 32 + 16 * h : 48 + 16 * h, LANES * y : LANES * (y + 1)] = (
                    solved - high.astype(F32)
                ).astype(BF16)
        mixed = jnp.dot(weights[f], x_s[f], preferred_element_type=F32)
        mixed = mixed[0:32] + mixed[32:64]
        for y in range(ROWS):
            rows = pl.ds(y, LEV, stride=ROWS)
            out[f, rows, :] = mixed[0:LEV, LANES * y : LANES * (y + 1)] * ocean_s[rows, :]

    for halo in halos:
        halo.wait_send()

    @pl.when(lat != ENDS)
    def _():
        to_ends(msg_ge, got_ge, 0).wait_send()
        to_ends(msg_pe, got_pe, 1).wait_send()

    @pl.when(lat == ENDS)
    def _():
        total(msg_fe.at[pl.ds(0, others)], e_ss.at[2], e_rs.at[2]).wait_send()

    @pl.when(solver)
    def _():
        total(msg_g.at[pl.ds(0, HALF - 1)], g_ss, g_rs).wait_send()
        total(msg_p.at[pl.ds(0, HALF - 1)], p_ss, p_rs).wait_send()
        total(msg_f.at[pl.ds(0, others)], f_ss, f_rs).wait_send()

    @pl.when(jnp.logical_not(solver))
    def _():
        total(msg_g.at[pl.ds(0, HALF)], g_ss, g_rs).wait_send()
        total(msg_p.at[pl.ds(0, HALF)], p_ss, p_rs).wait_send()


def solution(mesh):
    n_lon, n_lat = mesh.shape["lon"], mesh.shape["lat"]

    def per_device(tracer, ocean_mask, kappa_lon, kappa_lat, vertical_root):
        cells = (LEV, ROWS, LANES)
        natural = (PAD * ROWS, LANES)
        rows = (ROWS, 2, 16, LANES)
        scratch = [
            (FIELDS,) + cells,
            (cells, jnp.int32),
            (cells, BF16),
            (cells, BF16),
            (LEV, FIELDS, LEV),
            (1 + FIELDS, 4, 8, ROWS, LANES),
            (2, 1 + FIELDS, ROWS, LANES),
            (2, 1 + FIELDS, ROWS, LANES),
            natural,
            (FIELDS,) + natural,
            (LEV * ROWS, LANES),
            rows, rows, rows, rows,
            (FIELDS,) + rows,
            (64, LANES), (64, LANES),
            (ROWS, ROWS, LANES), (ROWS, ROWS, LANES),
            (HALF, 10, LANES), (n_lat, 10, LANES),
            (HALF, ROWS, LANES), (n_lat, ROWS, LANES),
            (n_lat, ROWS, LANES), (16, ROWS, LANES),
            (5, 4, LANES), (n_lat, 5, 4, LANES),
            (2, ROWS, LANES), (n_lat, 2, ROWS, LANES),
            (n_lat, 2, ROWS, LANES), (2, ROWS, LANES),
            (n_lat - 1, 3, 4, LANES),
            (n_lat - 1, 3, ROWS, LANES),
            (FIELDS, 32, LANES),
            ((FIELDS, 64, ROWS * LANES), BF16),
        ]
        scratch = [
            pltpu.VMEM(*item) if isinstance(item[0], tuple) else pltpu.VMEM(item, F32)
            for item in scratch
        ]
        sems = [(5,), (2,), (2,)] + [()] * 6 + [(3,)] * 2
        made = pl.pallas_call(
            functools.partial(kernel, n_lon, n_lat),
            out_shape=pltpu.VMEM((FIELDS, LEV * ROWS, LANES), F32),
            in_specs=[pl.BlockSpec(memory_space=pltpu.HBM)] * 5,
            out_specs=pl.BlockSpec(memory_space=pltpu.VMEM),
            scratch_shapes=scratch + [pltpu.SemaphoreType.DMA(shape) for shape in sems],
            compiler_params=pltpu.CompilerParams(
                collective_id=0, has_side_effects=True, vmem_limit_bytes=60 * 1024 * 1024
            ),
        )(tracer, ocean_mask, kappa_lon, kappa_lat, jnp.moveaxis(vertical_root, 0, 1))
        return made.reshape(FIELDS, LEV, ROWS, LANES)

    placed = (
        P(None, None, "lat", "lon"),
        P(None, "lat", "lon"),
        P(None, "lat", "lon"),
        P(None, "lat", "lon"),
        P(),
    )
    return jax.shard_map(
        per_device,
        mesh=mesh,
        in_specs=placed,
        out_specs=P(None, None, "lat", "lon"),
        check_vma=False,
    )
```

```python
import functools

import jax
import jax.numpy as jnp
from jax import lax
from jax.experimental import pallas as pl
from jax.experimental.pallas import tpu as pltpu
from jax.sharding import PartitionSpec as P

LEV = 25
FIELDS = 2
STEPS = 4
ROWS = 8
LANES = 128
HALF = 13
ENDS = 2
PAD = HALF + 16
STARTS = (0, 8, 13, 21)
COUNTS = (8, 5, 8, 4)
MESH = pl.DeviceIdType.MESH
F32 = jnp.float32
BF16 = jnp.bfloat16


def roll(cells, shift):
    return pltpu.roll(cells, shift % LANES, axis=cells.ndim - 1)


def pick(mask, yes, no):
    return jnp.where(jnp.broadcast_to(mask, yes.shape), yes, no)


def by_level(ref, row):
    return jnp.stack(
        [ref[pl.ds(half * HALF * ROWS + row, 16, stride=ROWS), :] for half in range(2)]
    )


def by_row(ref, row):
    return ref[pl.ds(row, ROWS, stride=ROWS), :]


def diffuse(state, face_east, face_west):
    for _ in range(STEPS):
        state = state + (
            face_east * (roll(state, -1) - state) - face_west * (state - roll(state, 1))
        )
    return state


def factor(coef):
    ones = jnp.ones_like(coef[0])
    excess = jnp.zeros_like(ones)
    ratio, ipiv, first = [], [], [ones]
    for y in range(ROWS - 1):
        face = jnp.minimum(coef[y], coef[y + 1])
        ipiv.append(1.0 / (1.0 + face + excess))
        ratio.append(face * ipiv[y])
        excess = ratio[y] * (1.0 + excess)
        first.append(ratio[y] * first[y])
    ipiv.append(1.0 / (1.0 + excess))
    g1, g8 = [first[-1] * ipiv[-1]], [ipiv[-1]]
    for y in reversed(range(ROWS - 1)):
        g1.append(first[y] * ipiv[y] + ratio[y] * g1[-1])
        g8.append(ratio[y] * g8[-1])
    return ratio, ipiv, g1[::-1], g8[::-1]


def kernel(
    n_lon, n_lat,
    tr_h, mk_h, kl_h, kt_h, vr_h, out,
    tr, mk, kl, kt, vr,
    lon_s, halo_out, halo_in, lat_s, diff_s, ocean_s,
    ratio_s, ipiv_s, g1_s, g8_s, part_s, edge_c, edge_s, edge_g1, edge_g8,
    msg_g, got_g, msg_p, got_p, msg_f, got_f,
    msg_ge, got_ge, msg_pe, got_pe, msg_fe, got_fe,
    line_s, line_e, vpad, x_s,
    in_sem, halo_ss, halo_rs, g_ss, g_rs, p_ss, p_rs, f_ss, f_rs, fe_ss, fe_rs, e_ss, e_rs, here,
):
    lon, lat = lax.axis_index("lon"), lax.axis_index("lat")
    east, west = lax.rem(lon + 1, n_lon), lax.rem(lon + n_lon - 1, n_lon)
    solver = lat < HALF

    loads = [
        pltpu.make_async_copy(src, dst, in_sem.at[i])
        for i, (src, dst) in enumerate(
            ((mk_h, mk), (kl_h, kl), (tr_h, tr), (kt_h, kt), (vr_h, vr))
        )
    ]
    for load in loads:
        load.start()

    barrier = pltpu.get_barrier_semaphore()
    pl.semaphore_signal(barrier, inc=1, device_id={"lon": west}, device_id_type=MESH)

    @pl.when(solver)
    def _():
        @pl.loop(1, n_lat)
        def _(d):
            pl.semaphore_signal(
                barrier, inc=1, device_id={"lat": lax.rem(lat + d, n_lat)}, device_id_type=MESH
            )

    lane = lax.broadcasted_iota(jnp.int32, (ROWS, LANES), 1)
    slot = (lane >> 2) & 3
    group = lane >> 4
    edge = (lane < 4) | (lane >= LANES - 4)

    got_f[HALF:16] = jnp.zeros((16 - HALF, ROWS, LANES), F32)
    vpad[...] = jnp.zeros(vpad.shape, F32)
    spare = pl.ds(LEV * ROWS, (PAD - LEV) * ROWS)
    lat_s[spare, :] = jnp.zeros(((PAD - LEV) * ROWS, LANES), F32)
    for f in range(FIELDS):
        diff_s[f, spare, :] = jnp.zeros(((PAD - LEV) * ROWS, LANES), F32)

    loads[0].wait()
    loads[1].wait()
    loads[2].wait()
    packed = []
    for t in range(4):
        n = COUNTS[t]
        levels = pl.ds(STARTS[t], n)
        ocean = mk[levels].astype(F32)
        ocean_s[pl.ds(STARTS[t] * ROWS, n * ROWS), :] = ocean.reshape(n * ROWS, LANES)
        lon_s[0, t, pl.ds(0, n)] = kl[levels].astype(F32) * ocean
        for f in range(FIELDS):
            lon_s[1 + f, t, pl.ds(0, n)] = tr[f, levels] * ocean
        tile = roll(lon_s[:, t, 0], 8)
        for g in range(1, n):
            tile = pick(group == 8 - g, roll(lon_s[:, t, g], 8 - 16 * g), tile)
        packed.append(tile)
    to_east, to_west = roll(packed[0], -4), roll(packed[0], -8)
    for t in range(1, 4):
        to_east = pick(slot == t, roll(packed[t], 4 * t - 4), to_east)
        to_west = pick(slot == t, roll(packed[t], 4 * t - 8), to_west)
    halo_out[0] = to_east
    halo_out[1] = to_west
    halos = [
        pltpu.make_async_remote_copy(
            src_ref=halo_out.at[i], dst_ref=halo_in.at[i],
            send_sem=halo_ss.at[i], recv_sem=halo_rs.at[i],
            device_id={"lon": side}, device_id_type=MESH,
        )
        for i, side in enumerate((east, west))
    ]

    @pl.when(solver)
    def _():
        pl.semaphore_wait(barrier, HALF)

    @pl.when(jnp.logical_not(solver))
    def _():
        pl.semaphore_wait(barrier, HALF + 1)

    halos[0].start()
    pl.semaphore_signal(here, inc=1, device_id={"lon": east}, device_id_type=MESH)

    def tile_to(msg, got, ss, rs, k):
        return pltpu.make_async_remote_copy(
            src_ref=msg.at[k], dst_ref=got.at[lat],
            send_sem=ss, recv_sem=rs, device_id={"lat": k}, device_id_type=MESH,
        )

    def send_to_solvers(msg, got, ss, rs):
        @pl.loop(1, n_lat)
        def _(d):
            k = lax.rem(lat + d, n_lat)

            @pl.when(k < HALF)
            def _():
                tile_to(msg, got, ss, rs, k).start()

        @pl.when(solver)
        def _():
            got[lat] = msg[lat]

    def total(ref, ss, rs):
        return pltpu.make_async_remote_copy(
            src_ref=ref, dst_ref=ref, send_sem=ss, recv_sem=rs,
            device_id={"lat": lax.rem(lat + 1, n_lat)}, device_id_type=MESH,
        )

    def to_ends(msg, got, kind, k):
        return pltpu.make_async_remote_copy(
            src_ref=msg, dst_ref=got.at[lat], send_sem=e_ss.at[kind, k], recv_sem=e_rs.at[kind],
            device_id={"lat": k}, device_id_type=MESH,
        )

    def of_ends(k):
        return pltpu.make_async_remote_copy(
            src_ref=msg_fe.at[k], dst_ref=got_fe, send_sem=fe_ss, recv_sem=fe_rs,
            device_id={"lat": k}, device_id_type=MESH,
        )

    def send_to_ends(msg, got, kind):
        for k in range(ENDS):

            @pl.when(lat != k)
            def _():
                to_ends(msg, got, kind, k).start()

            @pl.when(lat == k)
            def _():
                got[k] = msg[...]

    loads[3].wait()
    lat_s[pl.ds(0, LEV * ROWS), :] = kt[...].astype(F32).reshape(LEV * ROWS, LANES) * ocean_s[...]
    coef = [by_level(lat_s, y) for y in range(ROWS)]
    ratio, ipiv, g1, g8 = factor(coef)
    for y in range(ROWS):
        ipiv_s[y], g1_s[y], g8_s[y] = ipiv[y], g1[y], g8[y]
        if y < ROWS - 1:
            ratio_s[y] = ratio[y]
    for h in range(2):
        for q, value in enumerate((g1[0], g8[-1], g8[0], coef[0], coef[-1])):
            msg_g[:, 2 * q + h, :] = value[h, :HALF]
    send_to_solvers(msg_g, got_g, g_ss, g_rs)
    for t in range(4):
        tile = roll(lat_s[pl.ds(STARTS[t] * ROWS, ROWS), :], 8)
        for g in range(1, COUNTS[t]):
            tile = pick(
                group == 8 - g, roll(lat_s[pl.ds((STARTS[t] + g) * ROWS, ROWS), :], 8 - 16 * g), tile
            )
        for f in range(FIELDS):
            edge_c[pl.ds((4 * f + t) * ROWS, ROWS), :] = tile
    coef = [by_row(edge_c, y) for y in range(ROWS)]
    unused, unused, g1, g8 = factor(coef)
    for y in range(ROWS):
        edge_g1[y], edge_g8[y] = g1[y], g8[y]
    for q, value in enumerate((g1[0], g8[-1], g8[0], coef[0], coef[-1])):
        msg_ge[q] = value[0:4]
    send_to_ends(msg_ge, got_ge, 0)

    for t in range(4):
        n = COUNTS[t]
        coefs = lon_s[0, t, pl.ds(0, n)]
        face_east = jnp.minimum(coefs, roll(coefs, -1))
        face_west = roll(face_east, 1)
        for f in range(FIELDS):
            diff_s[f, pl.ds(STARTS[t] * ROWS, n * ROWS), :] = diffuse(
                lon_s[1 + f, t, pl.ds(0, n)], face_east, face_west
            ).reshape(n * ROWS, LANES)
    for f in range(FIELDS):
        p1 = p8 = jnp.zeros((2, 16, LANES), F32)
        for y in range(ROWS):
            value = by_level(diff_s.at[f], y)
            p1 = p1 + g1_s[y] * value
            p8 = p8 + g8_s[y] * value
        for h in range(2):
            msg_p[:, 2 * f + h, :] = p1[h, :HALF]
            msg_p[:, 4 + 2 * f + h, :] = p8[h, :HALF]
    send_to_solvers(msg_p, got_p, p_ss, p_rs)

    others = n_lat - 1

    def lines(face, own_first, own_last, cross, shape, keep):
        gamma = jnp.zeros(shape, F32)
        for m in range(others):
            low = cross(m)
            beta = face(m)
            beta = beta / (1.0 + beta * (own_first(m + 1) + (own_last(m) - low * gamma)))
            gamma = beta * cross(m + 1)
            for q, value in enumerate((beta, beta * low, gamma)):
                for ref in keep:
                    ref[m, q] = value

    def fluxes(jump, line, shape, put):
        flux = jnp.zeros(shape, F32)
        reduced = []
        for m in range(others):
            flux = line[m, 0] * jump(m) + line[m, 1] * flux
            reduced.append(flux)
        flux = jnp.zeros(shape, F32)
        put(others, 1, flux)
        put(0, 0, flux)
        for m in reversed(range(others)):
            flux = reduced[m] + line[m, 2] * flux
            put(m, 1, flux)
            put(m + 1, 0, flux)

    pl.semaphore_wait(here, 1)
    halos[1].start()
    for halo in halos:
        halo.wait_recv()
    from_west, from_east = halo_in[0], halo_in[1]
    edges = []
    for t in range(4):
        at_west = pick(slot == 1, roll(from_west, 4 - 4 * t), packed[t])
        at_east = pick(slot == 2, roll(from_east, 8 - 4 * t), packed[t])
        done = []
        for side in (at_west, at_east):
            face_east = jnp.minimum(side[0], roll(side[0], -1))
            done.append(diffuse(side[1:], face_east, roll(face_east, 1)))
        edges.append(pick((lane & 15) < 8, done[1], done[0]))
        for f in range(FIELDS):
            edge_s[pl.ds((4 * f + t) * ROWS, ROWS), :] = edges[t][f]
    p1 = p8 = jnp.zeros((ROWS, LANES), F32)
    for y in range(ROWS):
        value = by_row(edge_s, y)
        p1 = p1 + edge_g1[y] * value
        p8 = p8 + edge_g8[y] * value
    msg_pe[0] = p1
    msg_pe[1] = p8
    send_to_ends(msg_pe, got_pe, 1)

    @pl.when(solver)
    def _():
        total(got_g.at[pl.ds(0, others)], g_ss, g_rs).wait_recv()

        def part(q):
            return lambda b: got_g[b, 2 * q : 2 * q + 2, :]

        lines(
            lambda m: jnp.minimum(part(4)(m), part(3)(m + 1)), part(0), part(1), part(2),
            (2, LANES), [line_s.at[:, :, pl.ds(2 * f, 2)] for f in range(FIELDS)],
        )
        total(got_p.at[pl.ds(0, others)], p_ss, p_rs).wait_recv()

        def put(b, end, flux):
            msg_f[b, 4 * end : 4 * end + 4, :] = flux

        fluxes(
            lambda m: got_p[m + 1, 0:4, :] - got_p[m, 4:8, :], line_s, (4, LANES), put
        )

        @pl.loop(0, n_lat)
        def _(k):
            @pl.when(k != lat)
            def _():
                tile_to(msg_f, got_f, f_ss, f_rs, k).start()

        got_f[lat] = msg_f[lat]


    for t in range(4):
        for g in range(COUNTS[t]):
            rows = pl.ds((STARTS[t] + g) * ROWS, ROWS)
            ends = roll(edges[t], 16 * g - 8)
            for f in range(FIELDS):
                diff_s[f, rows, :] = jnp.where(edge, ends[f], diff_s[f, rows, :])
    for f in range(FIELDS):
        values = [by_level(diff_s.at[f], y) for y in range(ROWS)]
        for y in range(1, ROWS):
            values[y] = values[y] + ratio_s[y - 1] * values[y - 1]
        local = values[ROWS - 1] * ipiv_s[ROWS - 1]
        part_s[f, ROWS - 1] = local
        for y in reversed(range(ROWS - 1)):
            local = values[y] * ipiv_s[y] + ratio_s[y] * local
            part_s[f, y] = local
    loads[4].wait()
    col = lax.broadcasted_iota(jnp.int32, (32, LANES), 1)
    weights = []
    for f in range(FIELDS):
        vpad[f, 0:LEV, 0:LEV] = vr[:, f, :]
        root = vpad[f]
        root = jnp.where(col < HALF, root, 0.0) + jnp.where(
            (col >= 16) & (col < 16 + LEV - HALF), roll(root, 16 - HALF), 0.0
        )
        high = root.astype(BF16).astype(F32)
        stacked = jnp.concatenate([high, root - high], axis=0)
        weights.append((stacked + roll(stacked, 32)).astype(BF16)[:, :64])

    @pl.when(lat < ENDS)
    def _():
        total(got_ge.at[pl.ds(0, others)], e_ss.at[0, 0], e_rs.at[0]).wait_recv()
        lines(
            lambda m: jnp.minimum(got_ge[m, 4], got_ge[m + 1, 3]),
            lambda b: got_ge[b, 0], lambda b: got_ge[b, 1], lambda b: got_ge[b, 2],
            (4, LANES), [line_e.at[:, :, pl.ds(4 * f, 4)] for f in range(FIELDS)],
        )
        total(got_pe.at[pl.ds(0, others)], e_ss.at[1, 0], e_rs.at[1]).wait_recv()

        def put(b, end, flux):
            msg_fe[b, end] = flux

        fluxes(lambda m: got_pe[m + 1, 0] - got_pe[m, 1], line_e, (ROWS, LANES), put)
        got_fe[...] = msg_fe[lat]

    @pl.when(lat == 0)
    def _():
        @pl.loop(ENDS, n_lat)
        def _(k):
            of_ends(k).start()

    @pl.when(solver)
    def _():
        total(got_f.at[pl.ds(0, HALF - 1)], f_ss, f_rs).wait_recv()

    @pl.when(jnp.logical_not(solver))
    def _():
        total(got_f.at[pl.ds(0, HALF)], f_ss, f_rs).wait_recv()

    @pl.when(lat >= ENDS)
    def _():
        of_ends(lat).wait_recv()

    flux_e = roll(got_fe[...], -8)
    for f in range(FIELDS):
        for h in range(2):
            flux = []
            for end in range(2):
                inside = got_f[:, 4 * end + 2 * f + h, :]
                tiles = []
                for a in range(2):
                    row = 4 * f + 2 * h + a
                    ends = pltpu.roll(
                        jnp.broadcast_to(flux_e[end, row : row + 1], (ROWS, LANES)),
                        0, axis=1, stride=16, stride_axis=0,
                    )
                    tiles.append(
                        jnp.where(edge, ends, inside[ROWS * a : ROWS * (a + 1)])
                    )
                flux.append(jnp.concatenate(tiles, axis=0))
            for y in range(ROWS):
                solved = part_s[f, y, h] + (flux[1] * g8_s[y, h] - flux[0] * g1_s[y, h])
                high = solved.astype(BF16)
                x_s[f, 16 * h : 16 * h + 16, LANES * y : LANES * (y + 1)] = high
                x_s[f, 32 + 16 * h : 48 + 16 * h, LANES * y : LANES * (y + 1)] = (
                    solved - high.astype(F32)
                ).astype(BF16)
        mixed = jnp.dot(weights[f], x_s[f], preferred_element_type=F32)
        mixed = mixed[0:32] + mixed[32:64]
        for y in range(ROWS):
            rows = pl.ds(y, LEV, stride=ROWS)
            out[f, rows, :] = mixed[0:LEV, LANES * y : LANES * (y + 1)] * ocean_s[rows, :]

    for halo in halos:
        halo.wait_send()

    for k in range(ENDS):

        @pl.when(lat != k)
        def _():
            to_ends(msg_ge, got_ge, 0, k).wait_send()
            to_ends(msg_pe, got_pe, 1, k).wait_send()

    @pl.when(lat == 0)
    def _():
        total(msg_fe.at[pl.ds(0, n_lat - ENDS)], fe_ss, fe_rs).wait_send()

    @pl.when(solver)
    def _():
        total(msg_g.at[pl.ds(0, HALF - 1)], g_ss, g_rs).wait_send()
        total(msg_p.at[pl.ds(0, HALF - 1)], p_ss, p_rs).wait_send()
        total(msg_f.at[pl.ds(0, others)], f_ss, f_rs).wait_send()

    @pl.when(jnp.logical_not(solver))
    def _():
        total(msg_g.at[pl.ds(0, HALF)], g_ss, g_rs).wait_send()
        total(msg_p.at[pl.ds(0, HALF)], p_ss, p_rs).wait_send()


def solution(mesh):
    n_lon, n_lat = mesh.shape["lon"], mesh.shape["lat"]

    def per_device(tracer, ocean_mask, kappa_lon, kappa_lat, vertical_root):
        cells = (LEV, ROWS, LANES)
        natural = (PAD * ROWS, LANES)
        rows = (ROWS, 2, 16, LANES)
        scratch = [
            (FIELDS,) + cells,
            (cells, jnp.int32),
            (cells, BF16),
            (cells, BF16),
            (LEV, FIELDS, LEV),
            (1 + FIELDS, 4, 8, ROWS, LANES),
            (2, 1 + FIELDS, ROWS, LANES),
            (2, 1 + FIELDS, ROWS, LANES),
            natural,
            (FIELDS,) + natural,
            (LEV * ROWS, LANES),
            rows, rows, rows, rows,
            (FIELDS,) + rows,
            (64, LANES), (64, LANES),
            (ROWS, ROWS, LANES), (ROWS, ROWS, LANES),
            (HALF, 10, LANES), (n_lat, 10, LANES),
            (HALF, ROWS, LANES), (n_lat, ROWS, LANES),
            (n_lat, ROWS, LANES), (16, ROWS, LANES),
            (5, 4, LANES), (n_lat, 5, 4, LANES),
            (2, ROWS, LANES), (n_lat, 2, ROWS, LANES),
            (n_lat, 2, ROWS, LANES), (2, ROWS, LANES),
            (n_lat - 1, 3, 4, LANES),
            (n_lat - 1, 3, ROWS, LANES),
            (FIELDS, 32, LANES),
            ((FIELDS, 64, ROWS * LANES), BF16),
        ]
        scratch = [
            pltpu.VMEM(*item) if isinstance(item[0], tuple) else pltpu.VMEM(item, F32)
            for item in scratch
        ]
        sems = [(5,), (2,), (2,)] + [()] * 8 + [(2, ENDS), (2,)]
        made = pl.pallas_call(
            functools.partial(kernel, n_lon, n_lat),
            out_shape=pltpu.VMEM((FIELDS, LEV * ROWS, LANES), F32),
            in_specs=[pl.BlockSpec(memory_space=pltpu.HBM)] * 5,
            out_specs=pl.BlockSpec(memory_space=pltpu.VMEM),
            scratch_shapes=scratch
            + [pltpu.SemaphoreType.DMA(shape) for shape in sems]
            + [pltpu.SemaphoreType.REGULAR],
            compiler_params=pltpu.CompilerParams(
                collective_id=0, has_side_effects=True, vmem_limit_bytes=60 * 1024 * 1024
            ),
        )(tracer, ocean_mask, kappa_lon, kappa_lat, jnp.moveaxis(vertical_root, 0, 1))
        return made.reshape(FIELDS, LEV, ROWS, LANES)

    placed = (
        P(None, None, "lat", "lon"),
        P(None, "lat", "lon"),
        P(None, "lat", "lon"),
        P(None, "lat", "lon"),
        P(),
    )
    return jax.shard_map(
        per_device,
        mesh=mesh,
        in_specs=placed,
        out_specs=P(None, None, "lat", "lon"),
        check_vma=False,
    )
```

```python
import functools

import jax
import jax.numpy as jnp
from jax import lax
from jax.experimental import pallas as pl
from jax.experimental.pallas import tpu as pltpu
from jax.sharding import PartitionSpec as P

LEV = 25
FIELDS = 2
STEPS = 4
ROWS = 8
LANES = 128
HALF = 13
FEW = 7
TILES = 2 * FEW
RING, TOP = 8, 4
ENDS = 3
PAD = HALF + 16
STARTS = (0, 8, 13, 21)
COUNTS = (8, 5, 8, 4)
MESH = pl.DeviceIdType.MESH
F32 = jnp.float32
BF16 = jnp.bfloat16


def roll(cells, shift):
    return pltpu.roll(cells, shift % LANES, axis=cells.ndim - 1)


def pick(mask, yes, no):
    return jnp.where(jnp.broadcast_to(mask, yes.shape), yes, no)


def by_level(ref, row):
    return jnp.stack(
        [ref[pl.ds(half * HALF * ROWS + row, 16, stride=ROWS), :] for half in range(2)]
    )


def by_row(ref, row):
    return ref[pl.ds(row, ROWS, stride=ROWS), :]


def diffuse(state, face_east, face_west):
    for _ in range(STEPS):
        state = state + (
            face_east * (roll(state, -1) - state) - face_west * (state - roll(state, 1))
        )
    return state


def factor(coef):
    ones = jnp.ones_like(coef[0])
    excess = jnp.zeros_like(ones)
    ratio, ipiv, first = [], [], [ones]
    for y in range(ROWS - 1):
        face = jnp.minimum(coef[y], coef[y + 1])
        ipiv.append(1.0 / (1.0 + face + excess))
        ratio.append(face * ipiv[y])
        excess = ratio[y] * (1.0 + excess)
        first.append(ratio[y] * first[y])
    ipiv.append(1.0 / (1.0 + excess))
    g1, g8 = [first[-1] * ipiv[-1]], [ipiv[-1]]
    for y in reversed(range(ROWS - 1)):
        g1.append(first[y] * ipiv[y] + ratio[y] * g1[-1])
        g8.append(ratio[y] * g8[-1])
    return ratio, ipiv, g1[::-1], g8[::-1]


def kernel(
    n_lon, n_lat,
    tr_h, mk_h, kl_h, kt_h, vr_h, out,
    tr, mk, kl, kt, vr,
    lon_s, halo_out, halo_in, lat_s, diff_s, ocean_s,
    ratio_s, ipiv_s, g1_s, g8_s, part_s, edge_c, edge_s, edge_g1, edge_g8,
    two_g, two_p, joint_s, msg_g, got_g, msg_p, got_p, msg_f, got_f, flux_s,
    msg_ge, got_ge, msg_pe, got_pe, msg_fe, got_fe,
    line_s, line_e, vpad, x_s,
    in_sem, halo_ss, halo_rs, g_ss, g_rs, p_ss, p_rs, f_ss, f_rs, fe_ss, fe_rs, e_ss, e_rs, two_ss, two_rs, here,
):
    lon, lat = lax.axis_index("lon"), lax.axis_index("lat")
    east, west = lax.rem(lon + 1, n_lon), lax.rem(lon + n_lon - 1, n_lon)
    last = lon == n_lon - 1
    hosts = jnp.where(last, FEW, TILES)
    solver = lat < hosts
    core, mate = lat & 1, lat ^ 1
    own = (
        (jnp.logical_not(solver), 0),
        (solver & jnp.logical_not(last), 1),
        (solver & last, 2),
    )

    loads = [
        pltpu.make_async_copy(src, dst, in_sem.at[i])
        for i, (src, dst) in enumerate(
            ((mk_h, mk), (kl_h, kl), (tr_h, tr), (kt_h, kt), (vr_h, vr))
        )
    ]
    for load in loads:
        load.start()

    at = lax.rem(lon, RING)
    early = (at >= TOP, (at >= 1) & (at <= TOP))
    late = (at < TOP, (at > TOP) | (at == 0))
    barrier = pltpu.get_barrier_semaphore()
    for side, is_late in zip((east, west), late):

        @pl.when(is_late)
        def _():
            pl.semaphore_signal(barrier, inc=1, device_id={"lon": side}, device_id_type=MESH)

    @pl.when(solver)
    def _():
        @pl.loop(1, n_lat)
        def _(d):
            pl.semaphore_signal(
                barrier, inc=1, device_id={"lat": lax.rem(lat + d, n_lat)}, device_id_type=MESH
            )

    @pl.when(jnp.logical_not(solver))
    def _():
        pl.semaphore_signal(barrier, inc=1, device_id={"lat": mate}, device_id_type=MESH)

    others, chips = n_lat - 1, n_lat // 2
    lane = lax.broadcasted_iota(jnp.int32, (ROWS, LANES), 1)
    slot = (lane >> 2) & 3
    group = lane >> 4
    edge = (lane < 4) | (lane >= LANES - 4)

    flux_s[TILES:16] = jnp.zeros((16 - TILES, ROWS, LANES), F32)
    two_g[core, HALF:TILES] = jnp.zeros((TILES - HALF, 10, LANES), F32)
    two_p[core, HALF:TILES] = jnp.zeros((TILES - HALF, ROWS, LANES), F32)
    vpad[...] = jnp.zeros(vpad.shape, F32)
    spare = pl.ds(LEV * ROWS, (PAD - LEV) * ROWS)
    lat_s[spare, :] = jnp.zeros(((PAD - LEV) * ROWS, LANES), F32)
    for f in range(FIELDS):
        diff_s[f, spare, :] = jnp.zeros(((PAD - LEV) * ROWS, LANES), F32)

    loads[0].wait()
    loads[1].wait()
    loads[2].wait()
    packed = []
    for t in range(4):
        n = COUNTS[t]
        levels = pl.ds(STARTS[t], n)
        ocean = mk[levels].astype(F32)
        ocean_s[pl.ds(STARTS[t] * ROWS, n * ROWS), :] = ocean.reshape(n * ROWS, LANES)
        lon_s[0, t, pl.ds(0, n)] = kl[levels].astype(F32) * ocean
        for f in range(FIELDS):
            lon_s[1 + f, t, pl.ds(0, n)] = tr[f, levels] * ocean
        tile = roll(lon_s[:, t, 0], 8)
        for g in range(1, n):
            tile = pick(group == 8 - g, roll(lon_s[:, t, g], 8 - 16 * g), tile)
        packed.append(tile)
    to_east, to_west = roll(packed[0], -4), roll(packed[0], -8)
    for t in range(1, 4):
        to_east = pick(slot == t, roll(packed[t], 4 * t - 4), to_east)
        to_west = pick(slot == t, roll(packed[t], 4 * t - 8), to_west)
    halo_out[0] = to_east
    halo_out[1] = to_west
    halos = [
        pltpu.make_async_remote_copy(
            src_ref=halo_out.at[i], dst_ref=halo_in.at[i],
            send_sem=halo_ss.at[i], recv_sem=halo_rs.at[i],
            device_id={"lon": side}, device_id_type=MESH,
        )
        for i, side in enumerate((east, west))
    ]

    count = hosts - solver.astype(jnp.int32) + (mate >= hosts).astype(jnp.int32)
    for is_early in early:
        count = count + is_early.astype(jnp.int32)
    pl.semaphore_wait(barrier, count)
    for i in range(2):

        @pl.when(early[i])
        def _():
            halos[i].start()
            pl.semaphore_signal(
                here.at[1 - i], inc=1, device_id={"lon": (east, west)[i]}, device_id_type=MESH
            )

    def send_to_hosts(msg, got, ss, rs):
        for j in range(FEW):
            tile = 2 * j + core
            host = jnp.where(last, j, tile)
            place = jnp.where(last, core, 0) * chips + (lat >> 1)

            @pl.when(lat != host)
            def _():
                pltpu.make_async_remote_copy(
                    src_ref=msg.at[tile], dst_ref=got.at[place],
                    send_sem=ss, recv_sem=rs, device_id={"lat": host}, device_id_type=MESH,
                ).start()

            @pl.when(lat == host)
            def _():
                got[place] = msg[tile]

    def flux_tile(place):
        return jnp.where(last, 2 * lat + place, lat)

    def flux_to(place, k):
        return pltpu.make_async_remote_copy(
            src_ref=msg_f.at[place, k], dst_ref=got_f.at[flux_tile(place)],
            send_sem=f_ss, recv_sem=f_rs, device_id={"lat": k}, device_id_type=MESH,
        )

    def to_mate(ref, ss, rs):
        return pltpu.make_async_remote_copy(
            src_ref=ref.at[core], dst_ref=ref.at[core],
            send_sem=ss, recv_sem=rs, device_id={"lat": mate}, device_id_type=MESH,
        )

    def total(ref, ss, rs):
        return pltpu.make_async_remote_copy(
            src_ref=ref, dst_ref=ref, send_sem=ss, recv_sem=rs,
            device_id={"lat": lax.rem(lat + 1, n_lat)}, device_id_type=MESH,
        )

    def to_ends(msg, got, kind, k):
        return pltpu.make_async_remote_copy(
            src_ref=msg, dst_ref=got.at[lat], send_sem=e_ss.at[kind, k], recv_sem=e_rs.at[kind],
            device_id={"lat": k}, device_id_type=MESH,
        )

    def of_ends(k):
        return pltpu.make_async_remote_copy(
            src_ref=msg_fe.at[k], dst_ref=got_fe, send_sem=fe_ss, recv_sem=fe_rs,
            device_id={"lat": k}, device_id_type=MESH,
        )

    def send_to_ends(msg, got, kind):
        for k in (1, 0, 2):

            @pl.when(lat != k)
            def _():
                to_ends(msg, got, kind, k).start()

            @pl.when(lat == k)
            def _():
                got[k] = msg[...]

    loads[3].wait()
    lat_s[pl.ds(0, LEV * ROWS), :] = kt[...].astype(F32).reshape(LEV * ROWS, LANES) * ocean_s[...]
    coef = [by_level(lat_s, y) for y in range(ROWS)]
    ratio, ipiv, g1, g8 = factor(coef)
    for y in range(ROWS):
        ipiv_s[y], g1_s[y], g8_s[y] = ipiv[y], g1[y], g8[y]
        if y < ROWS - 1:
            ratio_s[y] = ratio[y]
    for h in range(2):
        for q, value in enumerate((g1[0], g8[-1], g8[0], coef[0], coef[-1])):
            two_g[core, 0:HALF, 2 * q + h, :] = value[h, :HALF]
    to_mate(two_g, two_ss.at[0], two_rs.at[0]).start()
    for t in range(4):
        tile = roll(lat_s[pl.ds(STARTS[t] * ROWS, ROWS), :], 8)
        for g in range(1, COUNTS[t]):
            tile = pick(
                group == 8 - g, roll(lat_s[pl.ds((STARTS[t] + g) * ROWS, ROWS), :], 8 - 16 * g), tile
            )
        for f in range(FIELDS):
            edge_c[pl.ds((4 * f + t) * ROWS, ROWS), :] = tile
    coef = [by_row(edge_c, y) for y in range(ROWS)]
    unused, unused, g1, g8 = factor(coef)
    for y in range(ROWS):
        edge_g1[y], edge_g8[y] = g1[y], g8[y]
    for q, value in enumerate((g1[0], g8[-1], g8[0], coef[0], coef[-1])):
        msg_ge[q] = value[0:4]

    for t in range(4):
        n = COUNTS[t]
        coefs = lon_s[0, t, pl.ds(0, n)]
        face_east = jnp.minimum(coefs, roll(coefs, -1))
        face_west = roll(face_east, 1)
        for f in range(FIELDS):
            diff_s[f, pl.ds(STARTS[t] * ROWS, n * ROWS), :] = diffuse(
                lon_s[1 + f, t, pl.ds(0, n)], face_east, face_west
            ).reshape(n * ROWS, LANES)
    for f in range(FIELDS):
        p1 = p8 = jnp.zeros((2, 16, LANES), F32)
        for y in range(ROWS):
            value = by_level(diff_s.at[f], y)
            p1 = p1 + g1_s[y] * value
            p8 = p8 + g8_s[y] * value
        for h in range(2):
            two_p[core, 0:HALF, 2 * f + h, :] = p1[h, :HALF]
            two_p[core, 0:HALF, 4 + 2 * f + h, :] = p8[h, :HALF]

    to_mate(two_p, two_ss.at[1], two_rs.at[1]).start()

    def lower(q):
        return two_g[0, :, 2 * q : 2 * q + 2, :]

    def upper(q):
        return two_g[1, :, 2 * q : 2 * q + 2, :]

    to_mate(two_g, two_ss.at[0], two_rs.at[0]).wait_recv()
    face = jnp.minimum(lower(4), upper(3))
    weight = face / (1.0 + face * (lower(1) + upper(0)))
    low_g, up_g = weight * lower(2), weight * upper(2)
    for q, value in enumerate(
        (lower(0) - low_g * lower(2), upper(1) - up_g * upper(2), low_g * upper(2), lower(3), upper(4))
    ):
        msg_g[:, 2 * q : 2 * q + 2, :] = value
    for f in range(FIELDS):
        for q, value in enumerate((weight, low_g, up_g)):
            joint_s[q, :, 2 * f : 2 * f + 2, :] = value
    send_to_hosts(msg_g, got_g, g_ss, g_rs)
    to_mate(two_p, two_ss.at[1], two_rs.at[1]).wait_recv()
    jump = two_p[1, :, 0:4, :] - two_p[0, :, 4:8, :]
    msg_p[:, 0:4, :] = two_p[0, :, 0:4, :] + joint_s[1] * jump
    msg_p[:, 4:8, :] = two_p[1, :, 4:8, :] - joint_s[2] * jump
    send_to_hosts(msg_p, got_p, p_ss, p_rs)
    send_to_ends(msg_ge, got_ge, 0)


    def lines(count, face, own_first, own_last, cross, shape, keep):
        gamma = jnp.zeros(shape, F32)
        for m in range(count):
            low = cross(m)
            beta = face(m)
            beta = beta / (1.0 + beta * (own_first(m + 1) + (own_last(m) - low * gamma)))
            gamma = beta * cross(m + 1)
            for q, value in enumerate((beta, beta * low, gamma)):
                for ref in keep:
                    ref[m, q] = value

    def fluxes(count, jump, line, shape, put):
        flux = jnp.zeros(shape, F32)
        reduced = []
        for m in range(count):
            flux = line[m, 0] * jump(m) + line[m, 1] * flux
            reduced.append(flux)
        flux = jnp.zeros(shape, F32)
        put(count, 1, flux)
        put(0, 0, flux)
        for m in reversed(range(count)):
            flux = reduced[m] + line[m, 2] * flux
            put(m, 1, flux)
            put(m + 1, 0, flux)

    for i in range(2):

        @pl.when(late[i])
        def _():
            pl.semaphore_wait(here.at[i], 1)
            halos[i].start()

    for halo in halos:
        halo.wait_recv()
    from_west, from_east = halo_in[0], halo_in[1]
    edges = []
    for t in range(4):
        at_west = pick(slot == 1, roll(from_west, 4 - 4 * t), packed[t])
        at_east = pick(slot == 2, roll(from_east, 8 - 4 * t), packed[t])
        done = []
        for side in (at_west, at_east):
            face_east = jnp.minimum(side[0], roll(side[0], -1))
            done.append(diffuse(side[1:], face_east, roll(face_east, 1)))
        edges.append(pick((lane & 15) < 8, done[1], done[0]))
        for f in range(FIELDS):
            edge_s[pl.ds((4 * f + t) * ROWS, ROWS), :] = edges[t][f]
    p1 = p8 = jnp.zeros((ROWS, LANES), F32)
    for y in range(ROWS):
        value = by_row(edge_s, y)
        p1 = p1 + edge_g1[y] * value
        p8 = p8 + edge_g8[y] * value
    msg_pe[...] = jnp.where((slot == 1) | (slot == 2), p1, roll(p8, 8))
    send_to_ends(msg_pe, got_pe, 1)

    def solve(places):
        def held(ref, b, rows):
            return jnp.stack([ref[chips * place + b, rows, :] for place in range(places)])

        def part(q):
            return lambda b: held(got_g, b, slice(2 * q, 2 * q + 2))

        count = chips * places - 1
        total(got_g.at[pl.ds(0, count)], g_ss, g_rs).wait_recv()
        lines(
            chips - 1, lambda m: jnp.minimum(part(4)(m), part(3)(m + 1)),
            part(0), part(1), part(2), (places, 2, LANES),
            [line_s.at[:, :, pl.ds(0, places), pl.ds(2 * f, 2)] for f in range(FIELDS)],
        )
        total(got_p.at[pl.ds(0, count)], p_ss, p_rs).wait_recv()

        def put(b, end, flux):
            for c in range(2):
                msg_f[0:places, 2 * b + c, 4 * end : 4 * end + 4, :] = flux

        fluxes(
            chips - 1, lambda m: held(got_p, m + 1, slice(0, 4)) - held(got_p, m, slice(4, 8)),
            line_s.at[:, :, pl.ds(0, places)], (places, 4, LANES), put,
        )

        @pl.loop(0, n_lat)
        def _(k):
            @pl.when(k != lat)
            def _():
                for place in range(places):
                    flux_to(place, k).start()

        for place in range(places):
            got_f[flux_tile(place)] = msg_f[place, lat]

    for holds, places in own[1:]:

        @pl.when(holds)
        def _():
            solve(places)

    for t in range(4):
        for g in range(COUNTS[t]):
            rows = pl.ds((STARTS[t] + g) * ROWS, ROWS)
            ends = roll(edges[t], 16 * g - 8)
            for f in range(FIELDS):
                diff_s[f, rows, :] = jnp.where(edge, ends[f], diff_s[f, rows, :])
    for f in range(FIELDS):
        values = [by_level(diff_s.at[f], y) for y in range(ROWS)]
        for y in range(1, ROWS):
            values[y] = values[y] + ratio_s[y - 1] * values[y - 1]
        local = values[ROWS - 1] * ipiv_s[ROWS - 1]
        part_s[f, ROWS - 1] = local
        for y in reversed(range(ROWS - 1)):
            local = values[y] * ipiv_s[y] + ratio_s[y] * local
            part_s[f, y] = local
    loads[4].wait()
    col = lax.broadcasted_iota(jnp.int32, (32, LANES), 1)
    weights = []
    for f in range(FIELDS):
        vpad[f, 0:LEV, 0:LEV] = vr[:, f, :]
        root = vpad[f]
        root = jnp.where(col < HALF, root, 0.0) + jnp.where(
            (col >= 16) & (col < 16 + LEV - HALF), roll(root, 16 - HALF), 0.0
        )
        high = root.astype(BF16).astype(F32)
        stacked = jnp.concatenate([high, root - high], axis=0)
        weights.append((stacked + roll(stacked, 32)).astype(BF16)[:, :64])

    @pl.when(lat < ENDS)
    def _():
        total(got_ge.at[pl.ds(0, others)], e_ss.at[0, 0], e_rs.at[0]).wait_recv()
        lines(
            others, lambda m: jnp.minimum(got_ge[m, 4], got_ge[m + 1, 3]),
            lambda b: got_ge[b, 0], lambda b: got_ge[b, 1], lambda b: got_ge[b, 2],
            (4, LANES), [line_e.at[:, :, pl.ds(4 * f, 4)] for f in range(FIELDS)],
        )
        total(got_pe.at[pl.ds(0, others)], e_ss.at[1, 0], e_rs.at[1]).wait_recv()

        def put(b, end, flux):
            msg_fe[b, end] = flux

        jumps = [got_pe[m + 1] - roll(got_pe[m], -8) for m in range(others)]
        fluxes(others, lambda m: jumps[m], line_e, (ROWS, LANES), put)
        got_fe[...] = msg_fe[lat]

    @pl.when(lat == ENDS - 1)
    def _():
        @pl.loop(ENDS, n_lat)
        def _(k):
            of_ends(k).start()

    for holds, places in own:

        @pl.when(holds)
        def _():
            total(got_f.at[pl.ds(0, TILES - places)], f_ss, f_rs).wait_recv()

    low, up = got_f[0:TILES, 0:4, :], got_f[0:TILES, 4:8, :]
    between = (
        joint_s[0] * (two_p[1, :, 0:4, :] - two_p[0, :, 4:8, :]) + joint_s[1] * low + joint_s[2] * up
    )
    flux_s[0:TILES, 0:4, :] = jnp.where(core == 0, low, between)
    flux_s[0:TILES, 4:8, :] = jnp.where(core == 0, between, up)

    @pl.when(lat >= ENDS)
    def _():
        of_ends(lat).wait_recv()

    flux_e = roll(got_fe[...], -8)
    for f in range(FIELDS):
        for h in range(2):
            flux = []
            for end in range(2):
                inside = flux_s[:, 4 * end + 2 * f + h, :]
                tiles = []
                for a in range(2):
                    row = 4 * f + 2 * h + a
                    ends = pltpu.roll(
                        jnp.broadcast_to(flux_e[end, row : row + 1], (ROWS, LANES)),
                        0, axis=1, stride=16, stride_axis=0,
                    )
                    tiles.append(
                        jnp.where(edge, ends, inside[ROWS * a : ROWS * (a + 1)])
                    )
                flux.append(jnp.concatenate(tiles, axis=0))
            for y in range(ROWS):
                solved = part_s[f, y, h] + (flux[1] * g8_s[y, h] - flux[0] * g1_s[y, h])
                high = solved.astype(BF16)
                x_s[f, 16 * h : 16 * h + 16, LANES * y : LANES * (y + 1)] = high
                x_s[f, 32 + 16 * h : 48 + 16 * h, LANES * y : LANES * (y + 1)] = (
                    solved - high.astype(F32)
                ).astype(BF16)
        mixed = jnp.dot(weights[f], x_s[f], preferred_element_type=F32)
        mixed = mixed[0:32] + mixed[32:64]
        for y in range(ROWS):
            rows = pl.ds(y, LEV, stride=ROWS)
            out[f, rows, :] = mixed[0:LEV, LANES * y : LANES * (y + 1)] * ocean_s[rows, :]

    for halo in halos:
        halo.wait_send()
    to_mate(two_g, two_ss.at[0], two_rs.at[0]).wait_send()
    to_mate(two_p, two_ss.at[1], two_rs.at[1]).wait_send()

    for k in range(ENDS):

        @pl.when(lat != k)
        def _():
            to_ends(msg_ge, got_ge, 0, k).wait_send()
            to_ends(msg_pe, got_pe, 1, k).wait_send()

    @pl.when(lat == ENDS - 1)
    def _():
        total(msg_fe.at[pl.ds(0, n_lat - ENDS)], fe_ss, fe_rs).wait_send()

    for holds, places in own:

        @pl.when(holds)
        def _():
            total(msg_g.at[pl.ds(0, FEW - min(places, 1))], g_ss, g_rs).wait_send()
            total(msg_p.at[pl.ds(0, FEW - min(places, 1))], p_ss, p_rs).wait_send()
            if places:
                total(msg_f.at[pl.ds(0, places), pl.ds(0, others)], f_ss, f_rs).wait_send()


def solution(mesh):
    n_lon, n_lat = mesh.shape["lon"], mesh.shape["lat"]

    def per_device(tracer, ocean_mask, kappa_lon, kappa_lat, vertical_root):
        cells = (LEV, ROWS, LANES)
        natural = (PAD * ROWS, LANES)
        rows = (ROWS, 2, 16, LANES)
        scratch = [
            (FIELDS,) + cells,
            (cells, jnp.int32),
            (cells, BF16),
            (cells, BF16),
            (LEV, FIELDS, LEV),
            (1 + FIELDS, 4, 8, ROWS, LANES),
            (2, 1 + FIELDS, ROWS, LANES),
            (2, 1 + FIELDS, ROWS, LANES),
            natural,
            (FIELDS,) + natural,
            (LEV * ROWS, LANES),
            rows, rows, rows, rows,
            (FIELDS,) + rows,
            (64, LANES), (64, LANES),
            (ROWS, ROWS, LANES), (ROWS, ROWS, LANES),
            (2, TILES, 10, LANES), (2, TILES, ROWS, LANES), (3, TILES, 4, LANES),
            (TILES, 10, LANES), (n_lat, 10, LANES),
            (TILES, ROWS, LANES), (n_lat, ROWS, LANES),
            (2, n_lat, ROWS, LANES), (TILES, ROWS, LANES), (16, ROWS, LANES),
            (5, 4, LANES), (n_lat, 5, 4, LANES),
            (ROWS, LANES), (n_lat, ROWS, LANES),
            (n_lat, 2, ROWS, LANES), (2, ROWS, LANES),
            (n_lat // 2 - 1, 3, 2, 4, LANES),
            (n_lat - 1, 3, ROWS, LANES),
            (FIELDS, 32, LANES),
            ((FIELDS, 64, ROWS * LANES), BF16),
        ]
        scratch = [
            pltpu.VMEM(*item) if isinstance(item[0], tuple) else pltpu.VMEM(item, F32)
            for item in scratch
        ]
        sems = [(5,), (2,), (2,)] + [()] * 8 + [(2, ENDS), (2,), (2,), (2,)]
        made = pl.pallas_call(
            functools.partial(kernel, n_lon, n_lat),
            out_shape=pltpu.VMEM((FIELDS, LEV * ROWS, LANES), F32),
            in_specs=[pl.BlockSpec(memory_space=pltpu.HBM)] * 5,
            out_specs=pl.BlockSpec(memory_space=pltpu.VMEM),
            scratch_shapes=scratch
            + [pltpu.SemaphoreType.DMA(shape) for shape in sems]
            + [pltpu.SemaphoreType.REGULAR((2,))],
            compiler_params=pltpu.CompilerParams(
                collective_id=0, has_side_effects=True, vmem_limit_bytes=60 * 1024 * 1024
            ),
        )(tracer, ocean_mask, kappa_lon, kappa_lat, jnp.moveaxis(vertical_root, 0, 1))
        return made.reshape(FIELDS, LEV, ROWS, LANES)

    placed = (
        P(None, None, "lat", "lon"),
        P(None, "lat", "lon"),
        P(None, "lat", "lon"),
        P(None, "lat", "lon"),
        P(),
    )
    return jax.shard_map(
        per_device,
        mesh=mesh,
        in_specs=placed,
        out_specs=P(None, None, "lat", "lon"),
        check_vma=False,
    )
```

```python
import functools

import jax
import jax.numpy as jnp
from jax import lax
from jax.experimental import pallas as pl
from jax.experimental.pallas import tpu as pltpu
from jax.sharding import PartitionSpec as P

LEV = 25
FIELDS = 2
STEPS = 4
ROWS = 8
LANES = 128
HALF = 13
FEW = 7
TILES = 2 * FEW
RING, TOP = 8, 4
ENDS = 3
PAD = HALF + 16
STARTS = (0, 8, 13, 21)
COUNTS = (8, 5, 8, 4)
MESH = pl.DeviceIdType.MESH
F32 = jnp.float32
BF16 = jnp.bfloat16


def roll(cells, shift):
    return pltpu.roll(cells, shift % LANES, axis=cells.ndim - 1)


def pick(mask, yes, no):
    return jnp.where(jnp.broadcast_to(mask, yes.shape), yes, no)


def by_level(ref, row):
    return jnp.stack(
        [ref[pl.ds(half * HALF * ROWS + row, 16, stride=ROWS), :] for half in range(2)]
    )


def by_row(ref, row):
    return ref[pl.ds(row, ROWS, stride=ROWS), :]


def diffuse(state, face_east, face_west):
    for _ in range(STEPS):
        state = state + (
            face_east * (roll(state, -1) - state) - face_west * (state - roll(state, 1))
        )
    return state


def factor(coef):
    ones = jnp.ones_like(coef[0])
    excess = jnp.zeros_like(ones)
    ratio, ipiv, first = [], [], [ones]
    for y in range(ROWS - 1):
        face = jnp.minimum(coef[y], coef[y + 1])
        ipiv.append(1.0 / (1.0 + face + excess))
        ratio.append(face * ipiv[y])
        excess = ratio[y] * (1.0 + excess)
        first.append(ratio[y] * first[y])
    ipiv.append(1.0 / (1.0 + excess))
    g1, g8 = [first[-1] * ipiv[-1]], [ipiv[-1]]
    for y in reversed(range(ROWS - 1)):
        g1.append(first[y] * ipiv[y] + ratio[y] * g1[-1])
        g8.append(ratio[y] * g8[-1])
    return ratio, ipiv, g1[::-1], g8[::-1]


def kernel(
    n_lon, n_lat,
    tr_h, mk_h, kl_h, kt_h, vr_h, out,
    tr, mk, kl, kt, vr,
    lon_s, halo_out, halo_in, lat_s, diff_s, ocean_s,
    ratio_s, ipiv_s, g1_s, g8_s, part_s, edge_c, edge_s, edge_g1, edge_g8,
    two_g, two_p, joint_s, msg_g, got_g, msg_p, got_p, msg_f, got_f, flux_s,
    msg_ge, got_ge, msg_pe, got_pe, msg_fe, got_fe,
    line_s, line_e, vpad, x_s,
    in_sem, halo_ss, halo_rs, g_ss, g_rs, p_ss, p_rs, f_ss, f_rs, fe_ss, fe_rs, e_ss, e_rs, two_ss, two_rs, here,
):
    lon, lat = lax.axis_index("lon"), lax.axis_index("lat")
    east, west = lax.rem(lon + 1, n_lon), lax.rem(lon + n_lon - 1, n_lon)
    last = lon == n_lon - 1
    hosts = jnp.where(last, FEW, TILES)
    solver = lat < hosts
    core, mate = lat & 1, lat ^ 1
    own = (
        (jnp.logical_not(solver), 0),
        (solver & jnp.logical_not(last), 1),
        (solver & last, 2),
    )

    loads = [
        pltpu.make_async_copy(src, dst, in_sem.at[i])
        for i, (src, dst) in enumerate(
            (
                (mk_h, mk), (kl_h, kl), (tr_h.at[0], tr.at[0]), (kt_h, kt), (vr_h, vr),
                (tr_h.at[1], tr.at[1]),
            )
        )
    ]
    for i in (2, 5, 0, 1, 3, 4):
        loads[i].start()

    at = lax.rem(lon, RING)
    early = (at >= TOP, (at >= 1) & (at <= TOP))
    late = (at < TOP, (at > TOP) | (at == 0))
    barrier = pltpu.get_barrier_semaphore()
    for side, is_late in zip((east, west), late):

        @pl.when(is_late)
        def _():
            pl.semaphore_signal(barrier, inc=1, device_id={"lon": side}, device_id_type=MESH)

    @pl.when(solver)
    def _():
        @pl.loop(1, n_lat)
        def _(d):
            pl.semaphore_signal(
                barrier, inc=1, device_id={"lat": lax.rem(lat + d, n_lat)}, device_id_type=MESH
            )

    @pl.when(jnp.logical_not(solver))
    def _():
        pl.semaphore_signal(barrier, inc=1, device_id={"lat": mate}, device_id_type=MESH)

    others, chips = n_lat - 1, n_lat // 2
    lane = lax.broadcasted_iota(jnp.int32, (ROWS, LANES), 1)
    slot = (lane >> 2) & 3
    group = lane >> 4
    edge = (lane < 4) | (lane >= LANES - 4)

    flux_s[TILES:16] = jnp.zeros((16 - TILES, ROWS, LANES), F32)
    two_g[core, HALF:TILES] = jnp.zeros((TILES - HALF, 10, LANES), F32)
    two_p[core, HALF:TILES] = jnp.zeros((TILES - HALF, ROWS, LANES), F32)
    vpad[...] = jnp.zeros(vpad.shape, F32)
    spare = pl.ds(LEV * ROWS, (PAD - LEV) * ROWS)
    lat_s[spare, :] = jnp.zeros(((PAD - LEV) * ROWS, LANES), F32)
    for f in range(FIELDS):
        diff_s[f, spare, :] = jnp.zeros(((PAD - LEV) * ROWS, LANES), F32)

    loads[0].wait()
    loads[1].wait()
    loads[2].wait()
    loads[5].wait()
    packed = []
    for t in range(4):
        n = COUNTS[t]
        levels = pl.ds(STARTS[t], n)
        ocean = mk[levels].astype(F32)
        ocean_s[pl.ds(STARTS[t] * ROWS, n * ROWS), :] = ocean.reshape(n * ROWS, LANES)
        lon_s[0, t, pl.ds(0, n)] = kl[levels].astype(F32) * ocean
        for f in range(FIELDS):
            lon_s[1 + f, t, pl.ds(0, n)] = tr[f, levels] * ocean
        tile = roll(lon_s[:, t, 0], 8)
        for g in range(1, n):
            tile = pick(group == 8 - g, roll(lon_s[:, t, g], 8 - 16 * g), tile)
        packed.append(tile)
    to_east, to_west = roll(packed[0], -4), roll(packed[0], -8)
    for t in range(1, 4):
        to_east = pick(slot == t, roll(packed[t], 4 * t - 4), to_east)
        to_west = pick(slot == t, roll(packed[t], 4 * t - 8), to_west)
    halo_out[0] = to_east
    halo_out[1] = to_west
    halos = [
        pltpu.make_async_remote_copy(
            src_ref=halo_out.at[i], dst_ref=halo_in.at[i],
            send_sem=halo_ss.at[i], recv_sem=halo_rs.at[i],
            device_id={"lon": side}, device_id_type=MESH,
        )
        for i, side in enumerate((east, west))
    ]

    count = hosts - solver.astype(jnp.int32) + (mate >= hosts).astype(jnp.int32)
    for is_early in early:
        count = count + is_early.astype(jnp.int32)
    pl.semaphore_wait(barrier, count)
    for i in range(2):

        @pl.when(early[i])
        def _():
            halos[i].start()
            pl.semaphore_signal(
                here.at[1 - i], inc=1, device_id={"lon": (east, west)[i]}, device_id_type=MESH
            )

    def send_to_hosts(msg, got, ss, rs):
        for j in range(FEW):
            tile = 2 * j + core
            host = jnp.where(last, j, tile)
            place = jnp.where(last, core, 0) * chips + (lat >> 1)

            @pl.when(lat != host)
            def _():
                pltpu.make_async_remote_copy(
                    src_ref=msg.at[tile], dst_ref=got.at[place],
                    send_sem=ss, recv_sem=rs, device_id={"lat": host}, device_id_type=MESH,
                ).start()

            @pl.when(lat == host)
            def _():
                got[place] = msg[tile]

    def flux_tile(place):
        return jnp.where(last, 2 * lat + place, lat)

    def flux_to(place, k):
        return pltpu.make_async_remote_copy(
            src_ref=msg_f.at[place, k], dst_ref=got_f.at[flux_tile(place)],
            send_sem=f_ss, recv_sem=f_rs, device_id={"lat": k}, device_id_type=MESH,
        )

    def to_mate(ref, ss, rs):
        return pltpu.make_async_remote_copy(
            src_ref=ref.at[core], dst_ref=ref.at[core],
            send_sem=ss, recv_sem=rs, device_id={"lat": mate}, device_id_type=MESH,
        )

    def total(ref, ss, rs):
        return pltpu.make_async_remote_copy(
            src_ref=ref, dst_ref=ref, send_sem=ss, recv_sem=rs,
            device_id={"lat": lax.rem(lat + 1, n_lat)}, device_id_type=MESH,
        )

    def to_ends(msg, got, kind, k):
        return pltpu.make_async_remote_copy(
            src_ref=msg, dst_ref=got.at[lat], send_sem=e_ss.at[kind, k], recv_sem=e_rs.at[kind],
            device_id={"lat": k}, device_id_type=MESH,
        )

    def of_ends(k):
        return pltpu.make_async_remote_copy(
            src_ref=msg_fe.at[k], dst_ref=got_fe, send_sem=fe_ss, recv_sem=fe_rs,
            device_id={"lat": k}, device_id_type=MESH,
        )

    def send_to_ends(msg, got, kind):
        for k in (1, 0, 2):

            @pl.when(lat != k)
            def _():
                to_ends(msg, got, kind, k).start()

            @pl.when(lat == k)
            def _():
                got[k] = msg[...]

    loads[3].wait()
    lat_s[pl.ds(0, LEV * ROWS), :] = kt[...].astype(F32).reshape(LEV * ROWS, LANES) * ocean_s[...]
    coef = [by_level(lat_s, y) for y in range(ROWS)]
    ratio, ipiv, g1, g8 = factor(coef)
    for y in range(ROWS):
        ipiv_s[y], g1_s[y], g8_s[y] = ipiv[y], g1[y], g8[y]
        if y < ROWS - 1:
            ratio_s[y] = ratio[y]
    for h in range(2):
        for q, value in enumerate((g1[0], g8[-1], g8[0], coef[0], coef[-1])):
            two_g[core, 0:HALF, 2 * q + h, :] = value[h, :HALF]
    to_mate(two_g, two_ss.at[0], two_rs.at[0]).start()
    for t in range(4):
        tile = roll(lat_s[pl.ds(STARTS[t] * ROWS, ROWS), :], 8)
        for g in range(1, COUNTS[t]):
            tile = pick(
                group == 8 - g, roll(lat_s[pl.ds((STARTS[t] + g) * ROWS, ROWS), :], 8 - 16 * g), tile
            )
        for f in range(FIELDS):
            edge_c[pl.ds((4 * f + t) * ROWS, ROWS), :] = tile
    coef = [by_row(edge_c, y) for y in range(ROWS)]
    unused, unused, g1, g8 = factor(coef)
    for y in range(ROWS):
        edge_g1[y], edge_g8[y] = g1[y], g8[y]
    for q, value in enumerate((g1[0], g8[-1], g8[0], coef[0], coef[-1])):
        msg_ge[q] = value[0:4]

    for t in range(4):
        n = COUNTS[t]
        coefs = lon_s[0, t, pl.ds(0, n)]
        face_east = jnp.minimum(coefs, roll(coefs, -1))
        face_west = roll(face_east, 1)
        for f in range(FIELDS):
            diff_s[f, pl.ds(STARTS[t] * ROWS, n * ROWS), :] = diffuse(
                lon_s[1 + f, t, pl.ds(0, n)], face_east, face_west
            ).reshape(n * ROWS, LANES)
    for f in range(FIELDS):
        p1 = p8 = jnp.zeros((2, 16, LANES), F32)
        for y in range(ROWS):
            value = by_level(diff_s.at[f], y)
            p1 = p1 + g1_s[y] * value
            p8 = p8 + g8_s[y] * value
        for h in range(2):
            two_p[core, 0:HALF, 2 * f + h, :] = p1[h, :HALF]
            two_p[core, 0:HALF, 4 + 2 * f + h, :] = p8[h, :HALF]

    to_mate(two_p, two_ss.at[1], two_rs.at[1]).start()

    def lower(q):
        return two_g[0, :, 2 * q : 2 * q + 2, :]

    def upper(q):
        return two_g[1, :, 2 * q : 2 * q + 2, :]

    to_mate(two_g, two_ss.at[0], two_rs.at[0]).wait_recv()
    face = jnp.minimum(lower(4), upper(3))
    weight = face / (1.0 + face * (lower(1) + upper(0)))
    low_g, up_g = weight * lower(2), weight * upper(2)
    for q, value in enumerate(
        (lower(0) - low_g * lower(2), upper(1) - up_g * upper(2), low_g * upper(2), lower(3), upper(4))
    ):
        msg_g[:, 2 * q : 2 * q + 2, :] = value
    for f in range(FIELDS):
        for q, value in enumerate((weight, low_g, up_g)):
            joint_s[q, :, 2 * f : 2 * f + 2, :] = value
    send_to_hosts(msg_g, got_g, g_ss, g_rs)
    to_mate(two_p, two_ss.at[1], two_rs.at[1]).wait_recv()
    jump = two_p[1, :, 0:4, :] - two_p[0, :, 4:8, :]
    msg_p[:, 0:4, :] = two_p[0, :, 0:4, :] + joint_s[1] * jump
    msg_p[:, 4:8, :] = two_p[1, :, 4:8, :] - joint_s[2] * jump
    send_to_hosts(msg_p, got_p, p_ss, p_rs)
    send_to_ends(msg_ge, got_ge, 0)


    def lines(count, face, own_first, own_last, cross, shape, keep):
        gamma = jnp.zeros(shape, F32)
        for m in range(count):
            low = cross(m)
            beta = face(m)
            beta = beta / (1.0 + beta * (own_first(m + 1) + (own_last(m) - low * gamma)))
            gamma = beta * cross(m + 1)
            for q, value in enumerate((beta, beta * low, gamma)):
                for ref in keep:
                    ref[m, q] = value

    def fluxes(count, jump, line, shape, put):
        flux = jnp.zeros(shape, F32)
        reduced = []
        for m in range(count):
            flux = line[m, 0] * jump(m) + line[m, 1] * flux
            reduced.append(flux)
        flux = jnp.zeros(shape, F32)
        put(count, 1, flux)
        put(0, 0, flux)
        for m in reversed(range(count)):
            flux = reduced[m] + line[m, 2] * flux
            put(m, 1, flux)
            put(m + 1, 0, flux)

    for i in range(2):

        @pl.when(late[i])
        def _():
            pl.semaphore_wait(here.at[i], 1)
            halos[i].start()

    for halo in halos:
        halo.wait_recv()
    from_west, from_east = halo_in[0], halo_in[1]
    edges = []
    for t in range(4):
        at_west = pick(slot == 1, roll(from_west, 4 - 4 * t), packed[t])
        at_east = pick(slot == 2, roll(from_east, 8 - 4 * t), packed[t])
        done = []
        for side in (at_west, at_east):
            face_east = jnp.minimum(side[0], roll(side[0], -1))
            done.append(diffuse(side[1:], face_east, roll(face_east, 1)))
        edges.append(pick((lane & 15) < 8, done[1], done[0]))
        for f in range(FIELDS):
            edge_s[pl.ds((4 * f + t) * ROWS, ROWS), :] = edges[t][f]
    p1 = p8 = jnp.zeros((ROWS, LANES), F32)
    for y in range(ROWS):
        value = by_row(edge_s, y)
        p1 = p1 + edge_g1[y] * value
        p8 = p8 + edge_g8[y] * value
    msg_pe[...] = jnp.where((slot == 1) | (slot == 2), p1, roll(p8, 8))
    send_to_ends(msg_pe, got_pe, 1)

    def solve(places):
        def held(ref, b, rows):
            return jnp.stack([ref[chips * place + b, rows, :] for place in range(places)])

        def part(q):
            return lambda b: held(got_g, b, slice(2 * q, 2 * q + 2))

        count = chips * places - 1
        total(got_g.at[pl.ds(0, count)], g_ss, g_rs).wait_recv()
        lines(
            chips - 1, lambda m: jnp.minimum(part(4)(m), part(3)(m + 1)),
            part(0), part(1), part(2), (places, 2, LANES),
            [line_s.at[:, :, pl.ds(0, places), pl.ds(2 * f, 2)] for f in range(FIELDS)],
        )
        total(got_p.at[pl.ds(0, count)], p_ss, p_rs).wait_recv()

        def put(b, end, flux):
            for c in range(2):
                msg_f[0:places, 2 * b + c, 4 * end : 4 * end + 4, :] = flux

        fluxes(
            chips - 1, lambda m: held(got_p, m + 1, slice(0, 4)) - held(got_p, m, slice(4, 8)),
            line_s.at[:, :, pl.ds(0, places)], (places, 4, LANES), put,
        )

        @pl.loop(0, n_lat)
        def _(k):
            @pl.when(k != lat)
            def _():
                for place in range(places):
                    flux_to(place, k).start()

        for place in range(places):
            got_f[flux_tile(place)] = msg_f[place, lat]

    for holds, places in own[1:]:

        @pl.when(holds)
        def _():
            solve(places)

    for t in range(4):
        for g in range(COUNTS[t]):
            rows = pl.ds((STARTS[t] + g) * ROWS, ROWS)
            ends = roll(edges[t], 16 * g - 8)
            for f in range(FIELDS):
                diff_s[f, rows, :] = jnp.where(edge, ends[f], diff_s[f, rows, :])
    for f in range(FIELDS):
        values = [by_level(diff_s.at[f], y) for y in range(ROWS)]
        for y in range(1, ROWS):
            values[y] = values[y] + ratio_s[y - 1] * values[y - 1]
        local = values[ROWS - 1] * ipiv_s[ROWS - 1]
        part_s[f, ROWS - 1] = local
        for y in reversed(range(ROWS - 1)):
            local = values[y] * ipiv_s[y] + ratio_s[y] * local
            part_s[f, y] = local
    loads[4].wait()
    col = lax.broadcasted_iota(jnp.int32, (32, LANES), 1)
    weights = []
    for f in range(FIELDS):
        vpad[f, 0:LEV, 0:LEV] = vr[:, f, :]
        root = vpad[f]
        root = jnp.where(col < HALF, root, 0.0) + jnp.where(
            (col >= 16) & (col < 16 + LEV - HALF), roll(root, 16 - HALF), 0.0
        )
        high = root.astype(BF16).astype(F32)
        stacked = jnp.concatenate([high, root - high], axis=0)
        weights.append((stacked + roll(stacked, 32)).astype(BF16)[:, :64])

    @pl.when(lat < ENDS)
    def _():
        total(got_ge.at[pl.ds(0, others)], e_ss.at[0, 0], e_rs.at[0]).wait_recv()
        lines(
            others, lambda m: jnp.minimum(got_ge[m, 4], got_ge[m + 1, 3]),
            lambda b: got_ge[b, 0], lambda b: got_ge[b, 1], lambda b: got_ge[b, 2],
            (4, LANES), [line_e.at[:, :, pl.ds(4 * f, 4)] for f in range(FIELDS)],
        )
        total(got_pe.at[pl.ds(0, others)], e_ss.at[1, 0], e_rs.at[1]).wait_recv()

        def put(b, end, flux):
            msg_fe[b, end] = flux

        jumps = [got_pe[m + 1] - roll(got_pe[m], -8) for m in range(others)]
        fluxes(others, lambda m: jumps[m], line_e, (ROWS, LANES), put)
        got_fe[...] = msg_fe[lat]

    @pl.when(lat == ENDS - 1)
    def _():
        @pl.loop(ENDS, n_lat)
        def _(k):
            of_ends(k).start()

    for holds, places in own:

        @pl.when(holds)
        def _():
            total(got_f.at[pl.ds(0, TILES - places)], f_ss, f_rs).wait_recv()

    low, up = got_f[0:TILES, 0:4, :], got_f[0:TILES, 4:8, :]
    between = (
        joint_s[0] * (two_p[1, :, 0:4, :] - two_p[0, :, 4:8, :]) + joint_s[1] * low + joint_s[2] * up
    )
    flux_s[0:TILES, 0:4, :] = jnp.where(core == 0, low, between)
    flux_s[0:TILES, 4:8, :] = jnp.where(core == 0, between, up)

    @pl.when(lat >= ENDS)
    def _():
        of_ends(lat).wait_recv()

    flux_e = roll(got_fe[...], -8)
    for f in range(FIELDS):
        for h in range(2):
            flux = []
            for end in range(2):
                inside = flux_s[:, 4 * end + 2 * f + h, :]
                tiles = []
                for a in range(2):
                    row = 4 * f + 2 * h + a
                    ends = pltpu.roll(
                        jnp.broadcast_to(flux_e[end, row : row + 1], (ROWS, LANES)),
                        0, axis=1, stride=16, stride_axis=0,
                    )
                    tiles.append(
                        jnp.where(edge, ends, inside[ROWS * a : ROWS * (a + 1)])
                    )
                flux.append(jnp.concatenate(tiles, axis=0))
            for y in range(ROWS):
                solved = part_s[f, y, h] + (flux[1] * g8_s[y, h] - flux[0] * g1_s[y, h])
                high = solved.astype(BF16)
                x_s[f, 16 * h : 16 * h + 16, LANES * y : LANES * (y + 1)] = high
                x_s[f, 32 + 16 * h : 48 + 16 * h, LANES * y : LANES * (y + 1)] = (
                    solved - high.astype(F32)
                ).astype(BF16)
        mixed = jnp.dot(weights[f], x_s[f], preferred_element_type=F32)
        mixed = mixed[0:32] + mixed[32:64]
        for y in range(ROWS):
            rows = pl.ds(y, LEV, stride=ROWS)
            out[f, rows, :] = mixed[0:LEV, LANES * y : LANES * (y + 1)] * ocean_s[rows, :]

    for halo in halos:
        halo.wait_send()
    to_mate(two_g, two_ss.at[0], two_rs.at[0]).wait_send()
    to_mate(two_p, two_ss.at[1], two_rs.at[1]).wait_send()

    for k in range(ENDS):

        @pl.when(lat != k)
        def _():
            to_ends(msg_ge, got_ge, 0, k).wait_send()
            to_ends(msg_pe, got_pe, 1, k).wait_send()

    @pl.when(lat == ENDS - 1)
    def _():
        total(msg_fe.at[pl.ds(0, n_lat - ENDS)], fe_ss, fe_rs).wait_send()

    for holds, places in own:

        @pl.when(holds)
        def _():
            total(msg_g.at[pl.ds(0, FEW - min(places, 1))], g_ss, g_rs).wait_send()
            total(msg_p.at[pl.ds(0, FEW - min(places, 1))], p_ss, p_rs).wait_send()
            if places:
                total(msg_f.at[pl.ds(0, places), pl.ds(0, others)], f_ss, f_rs).wait_send()


def solution(mesh):
    n_lon, n_lat = mesh.shape["lon"], mesh.shape["lat"]

    def per_device(tracer, ocean_mask, kappa_lon, kappa_lat, vertical_root):
        cells = (LEV, ROWS, LANES)
        natural = (PAD * ROWS, LANES)
        rows = (ROWS, 2, 16, LANES)
        scratch = [
            (FIELDS,) + cells,
            (cells, jnp.int32),
            (cells, BF16),
            (cells, BF16),
            (LEV, FIELDS, LEV),
            (1 + FIELDS, 4, 8, ROWS, LANES),
            (2, 1 + FIELDS, ROWS, LANES),
            (2, 1 + FIELDS, ROWS, LANES),
            natural,
            (FIELDS,) + natural,
            (LEV * ROWS, LANES),
            rows, rows, rows, rows,
            (FIELDS,) + rows,
            (64, LANES), (64, LANES),
            (ROWS, ROWS, LANES), (ROWS, ROWS, LANES),
            (2, TILES, 10, LANES), (2, TILES, ROWS, LANES), (3, TILES, 4, LANES),
            (TILES, 10, LANES), (n_lat, 10, LANES),
            (TILES, ROWS, LANES), (n_lat, ROWS, LANES),
            (2, n_lat, ROWS, LANES), (TILES, ROWS, LANES), (16, ROWS, LANES),
            (5, 4, LANES), (n_lat, 5, 4, LANES),
            (ROWS, LANES), (n_lat, ROWS, LANES),
            (n_lat, 2, ROWS, LANES), (2, ROWS, LANES),
            (n_lat // 2 - 1, 3, 2, 4, LANES),
            (n_lat - 1, 3, ROWS, LANES),
            (FIELDS, 32, LANES),
            ((FIELDS, 64, ROWS * LANES), BF16),
        ]
        scratch = [
            pltpu.VMEM(*item) if isinstance(item[0], tuple) else pltpu.VMEM(item, F32)
            for item in scratch
        ]
        sems = [(6,), (2,), (2,)] + [()] * 8 + [(2, ENDS), (2,), (2,), (2,)]
        made = pl.pallas_call(
            functools.partial(kernel, n_lon, n_lat),
            out_shape=pltpu.VMEM((FIELDS, LEV * ROWS, LANES), F32),
            in_specs=[pl.BlockSpec(memory_space=pltpu.HBM)] * 5,
            out_specs=pl.BlockSpec(memory_space=pltpu.VMEM),
            scratch_shapes=scratch
            + [pltpu.SemaphoreType.DMA(shape) for shape in sems]
            + [pltpu.SemaphoreType.REGULAR((2,))],
            compiler_params=pltpu.CompilerParams(
                collective_id=0, has_side_effects=True, vmem_limit_bytes=60 * 1024 * 1024
            ),
        )(tracer, ocean_mask, kappa_lon, kappa_lat, jnp.moveaxis(vertical_root, 0, 1))
        return made.reshape(FIELDS, LEV, ROWS, LANES)

    placed = (
        P(None, None, "lat", "lon"),
        P(None, "lat", "lon"),
        P(None, "lat", "lon"),
        P(None, "lat", "lon"),
        P(),
    )
    return jax.shard_map(
        per_device,
        mesh=mesh,
        in_specs=placed,
        out_specs=P(None, None, "lat", "lon"),
        check_vma=False,
    )
```

```python
import functools

import jax
import jax.numpy as jnp
from jax import lax
from jax.experimental import pallas as pl
from jax.experimental.pallas import tpu as pltpu
from jax.sharding import PartitionSpec as P

LEV = 25
FIELDS = 2
STEPS = 4
ROWS = 8
LANES = 128
HALF = 13
FEW = 7
TILES = 2 * FEW
RING, TOP = 8, 4
ENDS = 3
PAD = HALF + 16
STARTS = (0, 8, 13, 21)
COUNTS = (8, 5, 8, 4)
MESH = pl.DeviceIdType.MESH
F32 = jnp.float32
BF16 = jnp.bfloat16


def roll(cells, shift):
    return pltpu.roll(cells, shift % LANES, axis=cells.ndim - 1)


def pick(mask, yes, no):
    return jnp.where(jnp.broadcast_to(mask, yes.shape), yes, no)


def by_level(ref, row):
    return jnp.stack(
        [ref[pl.ds(half * HALF * ROWS + row, 16, stride=ROWS), :] for half in range(2)]
    )


def by_row(ref, row):
    return ref[pl.ds(row, ROWS, stride=ROWS), :]


def diffuse(state, face_east, face_west):
    for _ in range(STEPS):
        state = state + (
            face_east * (roll(state, -1) - state) - face_west * (state - roll(state, 1))
        )
    return state


def factor(coef):
    ones = jnp.ones_like(coef[0])
    excess = jnp.zeros_like(ones)
    ratio, ipiv, first = [], [], [ones]
    for y in range(ROWS - 1):
        face = jnp.minimum(coef[y], coef[y + 1])
        ipiv.append(1.0 / (1.0 + face + excess))
        ratio.append(face * ipiv[y])
        excess = ratio[y] * (1.0 + excess)
        first.append(ratio[y] * first[y])
    ipiv.append(1.0 / (1.0 + excess))
    g1, g8 = [first[-1] * ipiv[-1]], [ipiv[-1]]
    for y in reversed(range(ROWS - 1)):
        g1.append(first[y] * ipiv[y] + ratio[y] * g1[-1])
        g8.append(ratio[y] * g8[-1])
    return ratio, ipiv, g1[::-1], g8[::-1]


def kernel(
    n_lon, n_lat,
    tr_h, mk_h, kl_h, kt_h, vr_h, out,
    tr, mk, kl, kt, vr,
    lon_s, halo_out, halo_in, lat_s, diff_s, ocean_s,
    ratio_s, ipiv_s, g1_s, g8_s, part_s, edge_c, edge_s, edge_g1, edge_g8,
    two_g, two_p, joint_s, msg_g, got_g, msg_p, got_p, msg_f, got_f, flux_s,
    msg_ge, got_ge, msg_pe, got_pe, msg_fe, got_fe,
    line_s, line_e, vpad, x_s,
    in_sem, halo_ss, halo_rs, g_ss, g_rs, p_ss, p_rs, f_ss, f_rs, fe_ss, fe_rs, e_ss, e_rs, two_ss, two_rs, here,
):
    lon, lat = lax.axis_index("lon"), lax.axis_index("lat")
    east, west = lax.rem(lon + 1, n_lon), lax.rem(lon + n_lon - 1, n_lon)
    last = lon == n_lon - 1
    hosts = jnp.where(last, FEW, TILES)
    solver = lat < hosts
    core, mate = lat & 1, lat ^ 1
    own = (
        (jnp.logical_not(solver), 0),
        (solver & jnp.logical_not(last), 1),
        (solver & last, 2),
    )

    loads = [
        pltpu.make_async_copy(src, dst, in_sem.at[i])
        for i, (src, dst) in enumerate(
            ((mk_h, mk), (kl_h, kl), (tr_h, tr), (kt_h, kt), (vr_h, vr))
        )
    ]
    for load in loads:
        load.start()

    at = lax.rem(lon, RING)
    early = (at >= TOP, (at >= 1) & (at <= TOP))
    late = (at < TOP, (at > TOP) | (at == 0))
    barrier = pltpu.get_barrier_semaphore()
    for side, is_late in zip((east, west), late):

        @pl.when(is_late)
        def _():
            pl.semaphore_signal(barrier, inc=1, device_id={"lon": side}, device_id_type=MESH)

    @pl.when(solver)
    def _():
        @pl.loop(1, n_lat)
        def _(d):
            pl.semaphore_signal(
                barrier, inc=1, device_id={"lat": lax.rem(lat + d, n_lat)}, device_id_type=MESH
            )

    @pl.when(jnp.logical_not(solver))
    def _():
        pl.semaphore_signal(barrier, inc=1, device_id={"lat": mate}, device_id_type=MESH)

    others, chips = n_lat - 1, n_lat // 2
    lane = lax.broadcasted_iota(jnp.int32, (ROWS, LANES), 1)
    slot = (lane >> 2) & 3
    group = lane >> 4
    edge = (lane < 4) | (lane >= LANES - 4)

    flux_s[TILES:16] = jnp.zeros((16 - TILES, ROWS, LANES), F32)
    two_g[core, HALF:TILES] = jnp.zeros((TILES - HALF, 10, LANES), F32)
    two_p[core, HALF:TILES] = jnp.zeros((TILES - HALF, ROWS, LANES), F32)
    vpad[...] = jnp.zeros(vpad.shape, F32)
    spare = pl.ds(LEV * ROWS, (PAD - LEV) * ROWS)
    lat_s[spare, :] = jnp.zeros(((PAD - LEV) * ROWS, LANES), F32)
    for f in range(FIELDS):
        diff_s[f, spare, :] = jnp.zeros(((PAD - LEV) * ROWS, LANES), F32)

    loads[0].wait()
    loads[1].wait()
    loads[2].wait()
    packed = []
    for t in range(4):
        n = COUNTS[t]
        levels = pl.ds(STARTS[t], n)
        ocean = mk[levels].astype(F32)
        ocean_s[pl.ds(STARTS[t] * ROWS, n * ROWS), :] = ocean.reshape(n * ROWS, LANES)
        lon_s[0, t, pl.ds(0, n)] = kl[levels].astype(F32) * ocean
        for f in range(FIELDS):
            lon_s[1 + f, t, pl.ds(0, n)] = tr[f, levels] * ocean
        tile = roll(lon_s[:, t, 0], 8)
        for g in range(1, n):
            tile = pick(group == 8 - g, roll(lon_s[:, t, g], 8 - 16 * g), tile)
        packed.append(tile)
    to_east, to_west = roll(packed[0], -4), roll(packed[0], -8)
    for t in range(1, 4):
        to_east = pick(slot == t, roll(packed[t], 4 * t - 4), to_east)
        to_west = pick(slot == t, roll(packed[t], 4 * t - 8), to_west)
    halo_out[0] = to_east
    halo_out[1] = to_west
    halos = [
        pltpu.make_async_remote_copy(
            src_ref=halo_out.at[i], dst_ref=halo_in.at[i],
            send_sem=halo_ss.at[i], recv_sem=halo_rs.at[i],
            device_id={"lon": side}, device_id_type=MESH,
        )
        for i, side in enumerate((east, west))
    ]

    count = hosts - solver.astype(jnp.int32) + (mate >= hosts).astype(jnp.int32)
    for is_early in early:
        count = count + is_early.astype(jnp.int32)
    pl.semaphore_wait(barrier, count)
    for i in range(2):

        @pl.when(early[i])
        def _():
            halos[i].start()
            pl.semaphore_signal(
                here.at[1 - i], inc=1, device_id={"lon": (east, west)[i]}, device_id_type=MESH
            )

    def send_to_hosts(msg, got, ss, rs):
        for j in range(FEW):
            tile = 2 * j + core
            host = jnp.where(last, j, tile)
            place = jnp.where(last, core, 0) * chips + (lat >> 1)

            @pl.when(lat != host)
            def _():
                pltpu.make_async_remote_copy(
                    src_ref=msg.at[tile], dst_ref=got.at[place],
                    send_sem=ss, recv_sem=rs, device_id={"lat": host}, device_id_type=MESH,
                ).start()

            @pl.when(lat == host)
            def _():
                got[place] = msg[tile]

    def flux_tile(place):
        return jnp.where(last, 2 * lat + place, lat)

    def flux_to(place, k):
        return pltpu.make_async_remote_copy(
            src_ref=msg_f.at[place, k], dst_ref=got_f.at[flux_tile(place)],
            send_sem=f_ss, recv_sem=f_rs, device_id={"lat": k}, device_id_type=MESH,
        )

    def to_mate(ref, ss, rs):
        return pltpu.make_async_remote_copy(
            src_ref=ref.at[core], dst_ref=ref.at[core],
            send_sem=ss, recv_sem=rs, device_id={"lat": mate}, device_id_type=MESH,
        )

    def total(ref, ss, rs):
        return pltpu.make_async_remote_copy(
            src_ref=ref, dst_ref=ref, send_sem=ss, recv_sem=rs,
            device_id={"lat": lax.rem(lat + 1, n_lat)}, device_id_type=MESH,
        )

    def to_ends(msg, got, kind, k):
        return pltpu.make_async_remote_copy(
            src_ref=msg, dst_ref=got.at[lat], send_sem=e_ss.at[kind, k], recv_sem=e_rs.at[kind],
            device_id={"lat": k}, device_id_type=MESH,
        )

    def of_ends(k):
        return pltpu.make_async_remote_copy(
            src_ref=msg_fe.at[k], dst_ref=got_fe, send_sem=fe_ss, recv_sem=fe_rs,
            device_id={"lat": k}, device_id_type=MESH,
        )

    def send_to_ends(msg, got, kind):
        for k in (1, 0, 2):

            @pl.when(lat != k)
            def _():
                to_ends(msg, got, kind, k).start()

            @pl.when(lat == k)
            def _():
                got[k] = msg[...]

    loads[3].wait()
    lat_s[pl.ds(0, LEV * ROWS), :] = kt[...].astype(F32).reshape(LEV * ROWS, LANES) * ocean_s[...]
    coef = [by_level(lat_s, y) for y in range(ROWS)]
    ratio, ipiv, g1, g8 = factor(coef)
    for y in range(ROWS):
        ipiv_s[y], g1_s[y], g8_s[y] = ipiv[y], g1[y], g8[y]
        if y < ROWS - 1:
            ratio_s[y] = ratio[y]
    for h in range(2):
        for q, value in enumerate((g1[0], g8[-1], g8[0], coef[0], coef[-1])):
            two_g[core, 0:HALF, 2 * q + h, :] = value[h, :HALF]
    to_mate(two_g, two_ss.at[0], two_rs.at[0]).start()
    for t in range(4):
        n = COUNTS[t]
        coefs = lon_s[0, t, pl.ds(0, n)]
        face_east = jnp.minimum(coefs, roll(coefs, -1))
        face_west = roll(face_east, 1)
        for f in range(FIELDS):
            diff_s[f, pl.ds(STARTS[t] * ROWS, n * ROWS), :] = diffuse(
                lon_s[1 + f, t, pl.ds(0, n)], face_east, face_west
            ).reshape(n * ROWS, LANES)
    for f in range(FIELDS):
        p1 = p8 = jnp.zeros((2, 16, LANES), F32)
        for y in range(ROWS):
            value = by_level(diff_s.at[f], y)
            p1 = p1 + g1_s[y] * value
            p8 = p8 + g8_s[y] * value
        for h in range(2):
            two_p[core, 0:HALF, 2 * f + h, :] = p1[h, :HALF]
            two_p[core, 0:HALF, 4 + 2 * f + h, :] = p8[h, :HALF]

    to_mate(two_p, two_ss.at[1], two_rs.at[1]).start()


    def lower(q):
        return two_g[0, :, 2 * q : 2 * q + 2, :]

    def upper(q):
        return two_g[1, :, 2 * q : 2 * q + 2, :]

    to_mate(two_g, two_ss.at[0], two_rs.at[0]).wait_recv()
    face = jnp.minimum(lower(4), upper(3))
    weight = face / (1.0 + face * (lower(1) + upper(0)))
    low_g, up_g = weight * lower(2), weight * upper(2)
    for q, value in enumerate(
        (lower(0) - low_g * lower(2), upper(1) - up_g * upper(2), low_g * upper(2), lower(3), upper(4))
    ):
        msg_g[:, 2 * q : 2 * q + 2, :] = value
    for f in range(FIELDS):
        for q, value in enumerate((weight, low_g, up_g)):
            joint_s[q, :, 2 * f : 2 * f + 2, :] = value
    send_to_hosts(msg_g, got_g, g_ss, g_rs)

    for t in range(4):
        tile = roll(lat_s[pl.ds(STARTS[t] * ROWS, ROWS), :], 8)
        for g in range(1, COUNTS[t]):
            tile = pick(
                group == 8 - g, roll(lat_s[pl.ds((STARTS[t] + g) * ROWS, ROWS), :], 8 - 16 * g), tile
            )
        for f in range(FIELDS):
            edge_c[pl.ds((4 * f + t) * ROWS, ROWS), :] = tile
    coef = [by_row(edge_c, y) for y in range(ROWS)]
    unused, unused, g1, g8 = factor(coef)
    for y in range(ROWS):
        edge_g1[y], edge_g8[y] = g1[y], g8[y]
    for q, value in enumerate((g1[0], g8[-1], g8[0], coef[0], coef[-1])):
        msg_ge[q] = value[0:4]

    to_mate(two_p, two_ss.at[1], two_rs.at[1]).wait_recv()
    jump = two_p[1, :, 0:4, :] - two_p[0, :, 4:8, :]
    msg_p[:, 0:4, :] = two_p[0, :, 0:4, :] + joint_s[1] * jump
    msg_p[:, 4:8, :] = two_p[1, :, 4:8, :] - joint_s[2] * jump
    send_to_hosts(msg_p, got_p, p_ss, p_rs)
    send_to_ends(msg_ge, got_ge, 0)


    def lines(count, face, own_first, own_last, cross, shape, keep):
        gamma = jnp.zeros(shape, F32)
        for m in range(count):
            low = cross(m)
            beta = face(m)
            beta = beta / (1.0 + beta * (own_first(m + 1) + (own_last(m) - low * gamma)))
            gamma = beta * cross(m + 1)
            for q, value in enumerate((beta, beta * low, gamma)):
                for ref in keep:
                    ref[m, q] = value

    def fluxes(count, jump, line, shape, put):
        flux = jnp.zeros(shape, F32)
        reduced = []
        for m in range(count):
            flux = line[m, 0] * jump(m) + line[m, 1] * flux
            reduced.append(flux)
        flux = jnp.zeros(shape, F32)
        put(count, 1, flux)
        put(0, 0, flux)
        for m in reversed(range(count)):
            flux = reduced[m] + line[m, 2] * flux
            put(m, 1, flux)
            put(m + 1, 0, flux)

    for i in range(2):

        @pl.when(late[i])
        def _():
            pl.semaphore_wait(here.at[i], 1)
            halos[i].start()

    for halo in halos:
        halo.wait_recv()
    from_west, from_east = halo_in[0], halo_in[1]
    edges = []
    for t in range(4):
        at_west = pick(slot == 1, roll(from_west, 4 - 4 * t), packed[t])
        at_east = pick(slot == 2, roll(from_east, 8 - 4 * t), packed[t])
        done = []
        for side in (at_west, at_east):
            face_east = jnp.minimum(side[0], roll(side[0], -1))
            done.append(diffuse(side[1:], face_east, roll(face_east, 1)))
        edges.append(pick((lane & 15) < 8, done[1], done[0]))
        for f in range(FIELDS):
            edge_s[pl.ds((4 * f + t) * ROWS, ROWS), :] = edges[t][f]
    p1 = p8 = jnp.zeros((ROWS, LANES), F32)
    for y in range(ROWS):
        value = by_row(edge_s, y)
        p1 = p1 + edge_g1[y] * value
        p8 = p8 + edge_g8[y] * value
    msg_pe[...] = jnp.where((slot == 1) | (slot == 2), p1, roll(p8, 8))
    send_to_ends(msg_pe, got_pe, 1)

    def solve(places):
        def held(ref, b, rows):
            return jnp.stack([ref[chips * place + b, rows, :] for place in range(places)])

        def part(q):
            return lambda b: held(got_g, b, slice(2 * q, 2 * q + 2))

        count = chips * places - 1
        total(got_g.at[pl.ds(0, count)], g_ss, g_rs).wait_recv()
        lines(
            chips - 1, lambda m: jnp.minimum(part(4)(m), part(3)(m + 1)),
            part(0), part(1), part(2), (places, 2, LANES),
            [line_s.at[:, :, pl.ds(0, places), pl.ds(2 * f, 2)] for f in range(FIELDS)],
        )
        total(got_p.at[pl.ds(0, count)], p_ss, p_rs).wait_recv()

        def put(b, end, flux):
            for c in range(2):
                msg_f[0:places, 2 * b + c, 4 * end : 4 * end + 4, :] = flux

        fluxes(
            chips - 1, lambda m: held(got_p, m + 1, slice(0, 4)) - held(got_p, m, slice(4, 8)),
            line_s.at[:, :, pl.ds(0, places)], (places, 4, LANES), put,
        )

        @pl.loop(0, n_lat)
        def _(k):
            @pl.when(k != lat)
            def _():
                for place in range(places):
                    flux_to(place, k).start()

        for place in range(places):
            got_f[flux_tile(place)] = msg_f[place, lat]

    for holds, places in own[1:]:

        @pl.when(holds)
        def _():
            solve(places)

    for t in range(4):
        for g in range(COUNTS[t]):
            rows = pl.ds((STARTS[t] + g) * ROWS, ROWS)
            ends = roll(edges[t], 16 * g - 8)
            for f in range(FIELDS):
                diff_s[f, rows, :] = jnp.where(edge, ends[f], diff_s[f, rows, :])
    for f in range(FIELDS):
        values = [by_level(diff_s.at[f], y) for y in range(ROWS)]
        for y in range(1, ROWS):
            values[y] = values[y] + ratio_s[y - 1] * values[y - 1]
        local = values[ROWS - 1] * ipiv_s[ROWS - 1]
        part_s[f, ROWS - 1] = local
        for y in reversed(range(ROWS - 1)):
            local = values[y] * ipiv_s[y] + ratio_s[y] * local
            part_s[f, y] = local
    loads[4].wait()
    col = lax.broadcasted_iota(jnp.int32, (32, LANES), 1)
    weights = []
    for f in range(FIELDS):
        vpad[f, 0:LEV, 0:LEV] = vr[:, f, :]
        root = vpad[f]
        root = jnp.where(col < HALF, root, 0.0) + jnp.where(
            (col >= 16) & (col < 16 + LEV - HALF), roll(root, 16 - HALF), 0.0
        )
        high = root.astype(BF16).astype(F32)
        stacked = jnp.concatenate([high, root - high], axis=0)
        weights.append((stacked + roll(stacked, 32)).astype(BF16)[:, :64])

    @pl.when(lat < ENDS)
    def _():
        total(got_ge.at[pl.ds(0, others)], e_ss.at[0, 0], e_rs.at[0]).wait_recv()
        lines(
            others, lambda m: jnp.minimum(got_ge[m, 4], got_ge[m + 1, 3]),
            lambda b: got_ge[b, 0], lambda b: got_ge[b, 1], lambda b: got_ge[b, 2],
            (4, LANES), [line_e.at[:, :, pl.ds(4 * f, 4)] for f in range(FIELDS)],
        )
        total(got_pe.at[pl.ds(0, others)], e_ss.at[1, 0], e_rs.at[1]).wait_recv()

        def put(b, end, flux):
            msg_fe[b, end] = flux

        jumps = [got_pe[m + 1] - roll(got_pe[m], -8) for m in range(others)]
        fluxes(others, lambda m: jumps[m], line_e, (ROWS, LANES), put)
        got_fe[...] = msg_fe[lat]

    @pl.when(lat == ENDS - 1)
    def _():
        @pl.loop(ENDS, n_lat)
        def _(k):
            of_ends(k).start()

    for holds, places in own:

        @pl.when(holds)
        def _():
            total(got_f.at[pl.ds(0, TILES - places)], f_ss, f_rs).wait_recv()

    low, up = got_f[0:TILES, 0:4, :], got_f[0:TILES, 4:8, :]
    between = (
        joint_s[0] * (two_p[1, :, 0:4, :] - two_p[0, :, 4:8, :]) + joint_s[1] * low + joint_s[2] * up
    )
    flux_s[0:TILES, 0:4, :] = jnp.where(core == 0, low, between)
    flux_s[0:TILES, 4:8, :] = jnp.where(core == 0, between, up)

    @pl.when(lat >= ENDS)
    def _():
        of_ends(lat).wait_recv()

    flux_e = roll(got_fe[...], -8)
    for f in range(FIELDS):
        for h in range(2):
            flux = []
            for end in range(2):
                inside = flux_s[:, 4 * end + 2 * f + h, :]
                tiles = []
                for a in range(2):
                    row = 4 * f + 2 * h + a
                    ends = pltpu.roll(
                        jnp.broadcast_to(flux_e[end, row : row + 1], (ROWS, LANES)),
                        0, axis=1, stride=16, stride_axis=0,
                    )
                    tiles.append(
                        jnp.where(edge, ends, inside[ROWS * a : ROWS * (a + 1)])
                    )
                flux.append(jnp.concatenate(tiles, axis=0))
            for y in range(ROWS):
                solved = part_s[f, y, h] + (flux[1] * g8_s[y, h] - flux[0] * g1_s[y, h])
                high = solved.astype(BF16)
                x_s[f, 16 * h : 16 * h + 16, LANES * y : LANES * (y + 1)] = high
                x_s[f, 32 + 16 * h : 48 + 16 * h, LANES * y : LANES * (y + 1)] = (
                    solved - high.astype(F32)
                ).astype(BF16)
        mixed = jnp.dot(weights[f], x_s[f], preferred_element_type=F32)
        mixed = mixed[0:32] + mixed[32:64]
        for y in range(ROWS):
            rows = pl.ds(y, LEV, stride=ROWS)
            out[f, rows, :] = mixed[0:LEV, LANES * y : LANES * (y + 1)] * ocean_s[rows, :]

    for halo in halos:
        halo.wait_send()
    to_mate(two_g, two_ss.at[0], two_rs.at[0]).wait_send()
    to_mate(two_p, two_ss.at[1], two_rs.at[1]).wait_send()

    for k in range(ENDS):

        @pl.when(lat != k)
        def _():
            to_ends(msg_ge, got_ge, 0, k).wait_send()
            to_ends(msg_pe, got_pe, 1, k).wait_send()

    @pl.when(lat == ENDS - 1)
    def _():
        total(msg_fe.at[pl.ds(0, n_lat - ENDS)], fe_ss, fe_rs).wait_send()

    for holds, places in own:

        @pl.when(holds)
        def _():
            total(msg_g.at[pl.ds(0, FEW - min(places, 1))], g_ss, g_rs).wait_send()
            total(msg_p.at[pl.ds(0, FEW - min(places, 1))], p_ss, p_rs).wait_send()
            if places:
                total(msg_f.at[pl.ds(0, places), pl.ds(0, others)], f_ss, f_rs).wait_send()


def solution(mesh):
    n_lon, n_lat = mesh.shape["lon"], mesh.shape["lat"]

    def per_device(tracer, ocean_mask, kappa_lon, kappa_lat, vertical_root):
        cells = (LEV, ROWS, LANES)
        natural = (PAD * ROWS, LANES)
        rows = (ROWS, 2, 16, LANES)
        scratch = [
            (FIELDS,) + cells,
            (cells, jnp.int32),
            (cells, BF16),
            (cells, BF16),
            (LEV, FIELDS, LEV),
            (1 + FIELDS, 4, 8, ROWS, LANES),
            (2, 1 + FIELDS, ROWS, LANES),
            (2, 1 + FIELDS, ROWS, LANES),
            natural,
            (FIELDS,) + natural,
            (LEV * ROWS, LANES),
            rows, rows, rows, rows,
            (FIELDS,) + rows,
            (64, LANES), (64, LANES),
            (ROWS, ROWS, LANES), (ROWS, ROWS, LANES),
            (2, TILES, 10, LANES), (2, TILES, ROWS, LANES), (3, TILES, 4, LANES),
            (TILES, 10, LANES), (n_lat, 10, LANES),
            (TILES, ROWS, LANES), (n_lat, ROWS, LANES),
            (2, n_lat, ROWS, LANES), (TILES, ROWS, LANES), (16, ROWS, LANES),
            (5, 4, LANES), (n_lat, 5, 4, LANES),
            (ROWS, LANES), (n_lat, ROWS, LANES),
            (n_lat, 2, ROWS, LANES), (2, ROWS, LANES),
            (n_lat // 2 - 1, 3, 2, 4, LANES),
            (n_lat - 1, 3, ROWS, LANES),
            (FIELDS, 32, LANES),
            ((FIELDS, 64, ROWS * LANES), BF16),
        ]
        scratch = [
            pltpu.VMEM(*item) if isinstance(item[0], tuple) else pltpu.VMEM(item, F32)
            for item in scratch
        ]
        sems = [(5,), (2,), (2,)] + [()] * 8 + [(2, ENDS), (2,), (2,), (2,)]
        made = pl.pallas_call(
            functools.partial(kernel, n_lon, n_lat),
            out_shape=pltpu.VMEM((FIELDS, LEV * ROWS, LANES), F32),
            in_specs=[pl.BlockSpec(memory_space=pltpu.HBM)] * 5,
            out_specs=pl.BlockSpec(memory_space=pltpu.VMEM),
            scratch_shapes=scratch
            + [pltpu.SemaphoreType.DMA(shape) for shape in sems]
            + [pltpu.SemaphoreType.REGULAR((2,))],
            compiler_params=pltpu.CompilerParams(
                collective_id=0, has_side_effects=True, vmem_limit_bytes=60 * 1024 * 1024
            ),
        )(tracer, ocean_mask, kappa_lon, kappa_lat, jnp.moveaxis(vertical_root, 0, 1))
        return made.reshape(FIELDS, LEV, ROWS, LANES)

    placed = (
        P(None, None, "lat", "lon"),
        P(None, "lat", "lon"),
        P(None, "lat", "lon"),
        P(None, "lat", "lon"),
        P(),
    )
    return jax.shard_map(
        per_device,
        mesh=mesh,
        in_specs=placed,
        out_specs=P(None, None, "lat", "lon"),
        check_vma=False,
    )
```
